512 devices in a mesh: seq: 32 (over y, x_lo, core), chan: 16 (over z, x_hi).
Axes of the slice: x: 4 (x_hi: 2, x_lo: 2; x = x_hi * 2 + x_lo), y: 8, z: 8, core: 2. Of those that a mesh axis runs over, the one named last changes fastest.
Arguments:
- projected: bfloat16 [3, 4096, 4096], P(None, 'chan', 'seq'), may hold values from -6 to 6
- filters: float32 [4096, 4096], P('chan', 'seq'), may hold values from -8 to 8
- skip: float32 [4096], P('chan'), may hold values from -1 to 1
- out_weight: bfloat16 [4096, 8192], P(None, 'chan'), may hold values from -0.09375 to 0.09375
- cotangent: bfloat16 [4096, 8192], P('seq', 'chan'), may hold values from -1.5 to 1.5
Outputs:
- output: bfloat16 [4096, 8192], P('seq', 'chan')
- grads: bfloat16 [3, 4096, 4096], P(None, 'chan', 'seq')
The draws below stay inside these ranges and needn't reach their ends.
All inputs are finite; a program needn't handle non-finite values.
Results may differ from the reference program's by a relative error of at most 0.0049.
Values may be sent and summed in bfloat16 or wider, within the bound.
No kernel may reach another device: no remote copies, remote signals or barrier semaphores. Data moves between devices by JAX's collectives and lax.ppermute only.
A program may use at most 64 MiB of HBM per device.

```python
import math
import jax
import jax.numpy as jnp

D = 8192
FILTER_LANES = 4096
GENOME_LENGTH = 4096


def draw_filters(key, part):
    key = jax.random.fold_in(key, 7)
    generator_seeds = jax.random.split(key, 9)
    slow_share = 0.5
    slow = jax.random.bernoulli(generator_seeds[0], slow_share, (FILTER_LANES,))
    slow_rate = jnp.exp(jax.random.uniform(generator_seeds[1], (FILTER_LANES,), jnp.float32, math.log(0.1 / GENOME_LENGTH), math.log(2.0 / GENOME_LENGTH)))
    fast_rate = jnp.exp(jax.random.uniform(generator_seeds[2], (FILTER_LANES,), jnp.float32, math.log(1.0 / 50.0), math.log(1.0 / 30.0)))
    rate = jnp.where(slow, slow_rate, fast_rate)
    long_rate = jnp.exp(jax.random.uniform(generator_seeds[5], (FILTER_LANES,), jnp.float32, math.log(0.1 / GENOME_LENGTH), math.log(1.0 / GENOME_LENGTH)))
    long_share = jax.random.uniform(generator_seeds[6], (FILTER_LANES,), jnp.float32, 0.15, 0.4)
    channel_gain = jnp.exp(jax.random.uniform(generator_seeds[7], (FILTER_LANES,), jnp.float32, math.log(0.6), math.log(1.7)))
    lag_positions = jnp.arange(GENOME_LENGTH, dtype=jnp.int32)
    lag_float = lag_positions.astype(jnp.float32)[None, :]
    message_rounds = jax.random.randint(generator_seeds[3], (FILTER_LANES, 3), 1, GENOME_LENGTH)
    relayed_segments = jnp.sum((lag_positions[None, :, None] >= message_rounds[:, None, :]).astype(jnp.int32), axis=2)
    spike_occurrences = jnp.power(0.65, relayed_segments.astype(jnp.float32))
    main_scale = jnp.sqrt(2.0 * rate / -jnp.expm1(-2.0 * rate * GENOME_LENGTH))
    long_scale = jnp.sqrt(2.0 * long_rate / -jnp.expm1(-2.0 * long_rate * GENOME_LENGTH))
    leading_attenuation = jnp.exp(-rate[:, None] * lag_float) * (main_scale * jnp.sqrt(1.0 - long_share))[:, None]
    lingering_attenuation = jnp.exp(-long_rate[:, None] * lag_float) * (long_scale * jnp.sqrt(long_share))[:, None]
    leading_jitter = jax.random.truncated_normal(generator_seeds[4], -4.0, 4.0, (FILTER_LANES, GENOME_LENGTH), jnp.float32)
    lingering_jitter = jax.random.truncated_normal(generator_seeds[8], -4.0, 4.0, (FILTER_LANES, GENOME_LENGTH), jnp.float32)
    blended_kernel = (leading_attenuation * leading_jitter + lingering_attenuation * lingering_jitter) * spike_occurrences
    return (blended_kernel * channel_gain[:, None]).astype(jnp.float32)


def block_levels(stream_key, shape, cuts, low, top_value):
    def one(position, blocks):
        steps = jax.random.uniform(jax.random.fold_in(jax.random.fold_in(stream_key, 6), position), (blocks,), jnp.float32, low / len(cuts), top_value / len(cuts))
        return jnp.repeat(jnp.exp(steps), shape[position] // blocks).reshape((-1,) + (1,) * (len(shape) - position - 1))

    factor_of = one(*cuts[0])
    for cut in cuts[1:]:
        factor_of = factor_of * one(*cut)
    return factor_of


def scatter_about(rng, extent, deviation, bound, cuts=(), held_as=jnp.bfloat16):
    result = deviation * jax.random.normal(rng, extent, jnp.float32)
    if cuts:
        result = result * block_levels(rng, extent, cuts, -0.22, 0.18)
    return jnp.clip(result, -bound, bound).astype(held_as)


def setup_inputs(seed: int = 0) -> dict:
    splits = jax.random.split(jax.random.key(seed), 6)
    return {
        "projected": scatter_about(splits[0], (3, FILTER_LANES, GENOME_LENGTH), 1.0, 6.0, ((1, 16), (2, 32))),
        "filters": draw_filters(jax.random.fold_in(splits[5], 71), 0),
        "skip": jnp.clip(jax.random.uniform(splits[2], (FILTER_LANES,), jnp.float32, -1.0, 1.0) * block_levels(splits[2], (FILTER_LANES,), ((0, 16),), -0.4, 0.0), -1.0, 1.0),
        "out_weight": scatter_about(splits[3], (FILTER_LANES, D), FILTER_LANES ** -0.5, 0.09375, ((1, 16),)),
        "cotangent": scatter_about(splits[4], (GENOME_LENGTH, D), 0.25, 1.5, ((0, 32), (1, 16))),
    }


def causal_sum(signal, filters):
    length = signal.shape[-1]
    spectrum = jnp.fft.rfft(signal, n=2 * length) * jnp.fft.rfft(filters, n=2 * length)
    return jnp.fft.irfft(spectrum, n=2 * length)[:, :length]


def causal_adjoint(signal, filters):
    length = signal.shape[-1]
    spectrum = jnp.fft.rfft(signal, n=2 * length) * jnp.conj(jnp.fft.rfft(filters, n=2 * length))
    return jnp.fft.irfft(spectrum, n=2 * length)[:, :length]


def reference(projected, filters, skip, out_weight, cotangent):
    query = projected[0].astype(jnp.float32)
    key_in = projected[1].astype(jnp.float32)
    value = projected[2].astype(jnp.float32)
    mixed_in = key_in * value
    inner = causal_sum(mixed_in, filters) + skip[:, None] * mixed_in
    gated = (query * inner).astype(jnp.bfloat16)
    output = jnp.dot(gated.T, out_weight, preferred_element_type=jnp.float32).astype(jnp.bfloat16)
    grad_gated = jnp.dot(out_weight, cotangent.T, preferred_element_type=jnp.float32)
    grad_inner = grad_gated * query
    grad_mixed = causal_adjoint(grad_inner, filters) + skip[:, None] * grad_inner
    grads = jnp.stack([grad_gated * inner, grad_mixed * value, grad_mixed * key_in]).astype(jnp.bfloat16)
    return output, grads
```

```python
import jax
import jax.numpy as jnp
from jax import lax
from jax.experimental import pallas as pl
from jax.experimental.pallas import tpu as pltpu
from jax.sharding import PartitionSpec as P

BLOCK = 128
LANES = (((1,), (1,)), ((), ()))
ROWS = (((0,), (0,)), ((), ()))
VMEM_LIMIT = 32 << 20


def partial_half(half, weight, cotangent, received=None):
    planes, _, rows, width = weight.shape
    count = cotangent.shape[0]
    step = 2

    def kernel(half_ref, weight_ref, cotangent_ref, *refs):
        for plane in range(step):
            total = lax.dot_general(
                weight_ref[plane], cotangent_ref[...], LANES, preferred_element_type=jnp.float32
            )
            if received is not None:
                total = total + refs[0][plane].astype(jnp.float32)
            refs[-1][plane] = total.astype(jnp.bfloat16)

    block = pl.BlockSpec((step, rows, count), lambda i, half: (i, 0, 0))
    operands = [weight, cotangent] + ([] if received is None else [received])
    return pl.pallas_call(
        kernel,
        grid_spec=pltpu.PrefetchScalarGridSpec(
            num_scalar_prefetch=1,
            grid=(planes // step,),
            in_specs=[
                pl.BlockSpec((step, None, rows, width), lambda i, half: (i, half[0], 0, 0)),
                pl.BlockSpec((count, width), lambda i, half: (0, 0)),
            ]
            + ([] if received is None else [block]),
            out_specs=block,
        ),
        out_shape=jax.ShapeDtypeStruct((planes, rows, count), jnp.bfloat16),
        compiler_params=pltpu.CompilerParams(vmem_limit_bytes=VMEM_LIMIT),
        cost_estimate=pl.CostEstimate(
            flops=2 * planes * rows * width * count, bytes_accessed=4 << 20, transcendentals=0
        ),
        name="partial_grad_gated",
    )(half, *operands)


def project_half(half, gated, weight, before=None):
    planes, _, rows, width = weight.shape
    count = gated.shape[-1]
    step = 2
    last = planes // step - 1

    def kernel(half_ref, gated_ref, weight_ref, *refs):
        total_ref, out_ref = refs[-1], refs[-2]
        index = pl.program_id(0)

        @pl.when(index == 0)
        def _():
            if before is None:
                total_ref[...] = jnp.zeros_like(total_ref)
            else:
                total_ref[...] = refs[0][...]

        total = total_ref[...]
        for plane in range(step):
            total = total + lax.dot_general(
                gated_ref[plane], weight_ref[plane], ROWS, preferred_element_type=jnp.float32
            )
        total_ref[...] = total

        @pl.when(index == last)
        def _():
            out_ref[...] = total.astype(out_ref.dtype)

    whole = pl.BlockSpec((count, width), lambda i, half: (0, 0))
    operands = [gated, weight] + ([] if before is None else [before])
    return pl.pallas_call(
        kernel,
        grid_spec=pltpu.PrefetchScalarGridSpec(
            num_scalar_prefetch=1,
            grid=(planes // step,),
            in_specs=[
                pl.BlockSpec((step, rows, count), lambda i, half: (i, 0, 0)),
                pl.BlockSpec((step, None, rows, width), lambda i, half: (i, half[0], 0, 0)),
            ]
            + ([] if before is None else [whole]),
            out_specs=whole,
            scratch_shapes=[pltpu.VMEM((count, width), jnp.float32)],
        ),
        out_shape=jax.ShapeDtypeStruct(
            (count, width), jnp.float32 if before is None else jnp.bfloat16
        ),
        compiler_params=pltpu.CompilerParams(vmem_limit_bytes=VMEM_LIMIT),
        cost_estimate=pl.CostEstimate(
            flops=2 * planes * rows * width * count, bytes_accessed=4 << 20, transcendentals=0
        ),
        name="output_half",
    )(half, *operands)


def causal_kernel(
    skip_ref, given_ref, gated_ref, inner_ref, toeplitz_ref, wide, shifted, collected
):
    channel = pl.program_id(0)
    chunks, rows, _ = given_ref.shape
    per = rows // 4

    @pl.when(channel == 0)
    def _():
        wide[...] = given_ref[...].astype(jnp.float32).reshape(chunks * rows, BLOCK)
        shifted[pl.ds(0, chunks), :] = jnp.zeros((chunks, BLOCK), jnp.float32)

    def take(which):
        return wide[pl.ds(which * per + channel, chunks, stride=rows), :]

    query, mixed, taps = take(0), take(1) * take(2), take(3)
    shifted[pl.ds(chunks, chunks), :] = mixed
    upper = lax.broadcasted_iota(jnp.int32, (BLOCK, BLOCK), 1) >= lax.broadcasted_iota(
        jnp.int32, (BLOCK, BLOCK), 0
    )
    before = jnp.zeros((BLOCK, BLOCK), jnp.float32)
    total = jnp.zeros((chunks, BLOCK), jnp.float32)
    for lag in range(0, chunks, 2):
        blocks, signals = [], []
        for one in (lag, lag + 1):
            spread = jnp.broadcast_to(taps[one : one + 1, :], (BLOCK, BLOCK))
            turned = pltpu.roll(spread, 0, 1, stride=1, stride_axis=0)
            block = jnp.where(upper, turned, before).astype(jnp.bfloat16)
            before = turned
            toeplitz_ref[:, one * BLOCK : (one + 1) * BLOCK] = block
            blocks.append(block)
            signals.append(shifted[chunks - one : 2 * chunks - one, :].astype(jnp.bfloat16))
        total = total + jnp.dot(
            jnp.concatenate(signals, axis=1),
            jnp.concatenate(blocks, axis=0),
            preferred_element_type=jnp.float32,
        )
    inner = total + skip_ref[channel] * mixed
    inner_ref[...] = inner
    collected[pl.ds(channel, chunks, stride=per), :] = query * inner

    @pl.when(channel == per - 1)
    def _():
        gated_ref[...] = collected[...].astype(jnp.bfloat16).reshape(gated_ref.shape)


def causal(given, skip):
    chunks, rows, _ = given.shape
    per = rows // 4
    whole = pl.BlockSpec(memory_space=pltpu.SMEM)
    return pl.pallas_call(
        causal_kernel,
        grid=(per,),
        in_specs=[whole, pl.BlockSpec(given.shape, lambda c: (0, 0, 0))],
        out_specs=[
            pl.BlockSpec((chunks // 2, 2 * per, BLOCK), lambda c: (0, 0, 0)),
            pl.BlockSpec((None, chunks, BLOCK), lambda c: (c, 0, 0)),
            pl.BlockSpec((None, BLOCK, chunks * BLOCK), lambda c: (c, 0, 0)),
        ],
        out_shape=[
            jax.ShapeDtypeStruct((chunks // 2, 2 * per, BLOCK), jnp.bfloat16),
            jax.ShapeDtypeStruct((per, chunks, BLOCK), jnp.float32),
            jax.ShapeDtypeStruct((per, BLOCK, chunks * BLOCK), jnp.bfloat16),
        ],
        scratch_shapes=[
            pltpu.VMEM((chunks * rows, BLOCK), jnp.float32),
            pltpu.VMEM((2 * chunks, BLOCK), jnp.float32),
            pltpu.VMEM((chunks * per, BLOCK), jnp.float32),
        ],
        compiler_params=pltpu.CompilerParams(vmem_limit_bytes=VMEM_LIMIT),
        cost_estimate=pl.CostEstimate(
            flops=16 * per * chunks * chunks * BLOCK * BLOCK,
            bytes_accessed=16 << 20,
            transcendentals=0,
        ),
        name="causal_sum",
    )(skip, given)


def adjoint_kernel(
    skip_ref, given_ref, back_ref, inner_ref, toeplitz_ref, out_ref, wide, grads, shifted, collected
):
    channel = pl.program_id(0)
    chunks, rows, _ = given_ref.shape
    per = rows // 4

    @pl.when(channel == 0)
    def _():
        wide[...] = given_ref[...].astype(jnp.float32).reshape(chunks * rows, BLOCK)
        grads[...] = back_ref[...].astype(jnp.float32).reshape(chunks * 2 * per, BLOCK)
        shifted[pl.ds(chunks, chunks), :] = jnp.zeros((chunks, BLOCK), jnp.float32)

    def take(which):
        return wide[pl.ds(which * per + channel, chunks, stride=rows), :]

    query, key_in, value = take(0), take(1), take(2)
    grad_gated = grads[pl.ds(per + channel, chunks, stride=2 * per), :]
    grad_inner = grad_gated * query
    shifted[pl.ds(0, chunks), :] = grad_inner
    total = jnp.zeros((chunks, BLOCK), jnp.float32)
    for lag in range(0, chunks, 2):
        signals = [shifted[one : one + chunks, :] for one in (lag, lag + 1)]
        total = total + lax.dot_general(
            jnp.concatenate(signals, axis=1).astype(jnp.bfloat16),
            toeplitz_ref[:, lag * BLOCK : (lag + 2) * BLOCK],
            LANES,
            preferred_element_type=jnp.float32,
        )
    grad_mixed = total + skip_ref[channel] * grad_inner
    results = (grad_gated * inner_ref[...], grad_mixed * value, grad_mixed * key_in)
    for which, result in enumerate(results):
        collected[pl.ds(which * per + channel, chunks, stride=3 * per), :] = result

    @pl.when(channel == per - 1)
    def _():
        out_ref[...] = collected[...].astype(jnp.bfloat16).reshape(out_ref.shape)


def adjoint(given, back, inner, toeplitz, skip):
    chunks, rows, _ = given.shape
    per = rows // 4
    return pl.pallas_call(
        adjoint_kernel,
        grid=(per,),
        in_specs=[
            pl.BlockSpec(memory_space=pltpu.SMEM),
            pl.BlockSpec(given.shape, lambda c: (0, 0, 0)),
            pl.BlockSpec(back.shape, lambda c: (0, 0, 0)),
            pl.BlockSpec((None, chunks, BLOCK), lambda c: (c, 0, 0)),
            pl.BlockSpec((None, BLOCK, chunks * BLOCK), lambda c: (c, 0, 0)),
        ],
        out_specs=pl.BlockSpec((chunks // 2, 6 * per, BLOCK), lambda c: (0, 0, 0)),
        out_shape=jax.ShapeDtypeStruct((chunks // 2, 6 * per, BLOCK), jnp.bfloat16),
        scratch_shapes=[
            pltpu.VMEM((chunks * rows, BLOCK), jnp.float32),
            pltpu.VMEM((chunks * 2 * per, BLOCK), jnp.float32),
            pltpu.VMEM((2 * chunks, BLOCK), jnp.float32),
            pltpu.VMEM((chunks * 3 * per, BLOCK), jnp.float32),
        ],
        compiler_params=pltpu.CompilerParams(vmem_limit_bytes=VMEM_LIMIT),
        cost_estimate=pl.CostEstimate(
            flops=16 * per * chunks * chunks * BLOCK * BLOCK,
            bytes_accessed=16 << 20,
            transcendentals=0,
        ),
        name="adjoint_sum",
    )(skip, given, back, inner, toeplitz)


def per_device(projected, filters, skip, out_weight, cotangent):
    seq = lax.axis_size("seq")
    chan = lax.axis_size("chan")
    planes = chan // 2
    channels, count = filters.shape
    per = channels // seq
    half = lax.axis_index("chan") & 1
    own, other = half.reshape(1), (1 - half).reshape(1)
    along_z = [[2 * z + h for z in range(planes)] for h in range(2)]
    pairs = [(i, i ^ 1) for i in range(chan)]

    def exchange_seq(array):
        return lax.all_to_all(array, "seq", 0, 0, tiled=True)

    def exchange_z(array):
        return lax.all_to_all(array, "chan", 0, 0, tiled=True, axis_index_groups=along_z)

    weight = out_weight.reshape(planes, 2, channels, out_weight.shape[1])
    received = lax.ppermute(partial_half(other, weight, cotangent), "chan", pairs)
    sent = jnp.concatenate([projected, filters.astype(jnp.bfloat16)[None]]).reshape(
        4, seq, per, count
    )
    given = exchange_seq(sent.transpose(1, 0, 2, 3).reshape(seq, 4 * per, count))
    skip_here = lax.dynamic_slice(skip, (lax.axis_index("seq") * per,), (per,))
    gated, inner, toeplitz = causal(given, skip_here)
    shares = exchange_z(partial_half(own, weight, cotangent, received))
    grad_gated = jnp.sum(shares.astype(jnp.float32), axis=0).astype(jnp.bfloat16)
    middle = exchange_seq(
        jnp.concatenate(
            [gated.reshape(seq, per, count), grad_gated.reshape(seq, per, count)], axis=1
        )
    )
    gated_here = middle[:, :per].reshape(channels, count)
    gated_half = exchange_z(jnp.broadcast_to(gated_here[None], (planes, channels, count)))
    grads_there = adjoint(given, middle, inner, toeplitz, skip_here)
    gated_other = lax.ppermute(gated_half, "chan", pairs)
    grads_there, gated_half = lax.optimization_barrier((grads_there, gated_half))
    grads = exchange_seq(grads_there.reshape(seq, 3 * per, count))
    grads = grads.reshape(seq, 3, per, count).transpose(1, 0, 2, 3).reshape(3, channels, count)
    output = project_half(own, gated_half, weight)
    output = project_half(other, gated_other, weight, output)
    return output, grads


def solution(mesh):
    in_specs = (
        P(None, "chan", "seq"),
        P("chan", "seq"),
        P("chan"),
        P(None, "chan"),
        P("seq", "chan"),
    )
    out_specs = (P("seq", "chan"), P(None, "chan", "seq"))
    return jax.shard_map(
        per_device, mesh=mesh, in_specs=in_specs, out_specs=out_specs, check_vma=False
    )
```

```python
import jax
import jax.numpy as jnp
from jax import lax
from jax.experimental import pallas as pl
from jax.experimental.pallas import tpu as pltpu
from jax.sharding import PartitionSpec as P

BLOCK = 128
LANES = (((1,), (1,)), ((), ()))
ROWS = (((0,), (0,)), ((), ()))
VMEM_LIMIT = 8 << 20
FIRST_LIMIT = 54 << 20
VMEM = pl.BlockSpec(memory_space=pltpu.VMEM)
HBM = pl.BlockSpec(memory_space=pltpu.HBM)
SMEM = pl.BlockSpec(memory_space=pltpu.SMEM)


def call(kernel, in_specs, out_shape, flops, scratch=(), name=None, limit=VMEM_LIMIT):
    return pl.pallas_call(
        kernel,
        in_specs=in_specs,
        out_specs=jax.tree.map(lambda _: VMEM, out_shape),
        out_shape=out_shape,
        scratch_shapes=list(scratch),
        compiler_params=pltpu.CompilerParams(vmem_limit_bytes=limit),
        cost_estimate=pl.CostEstimate(flops=flops, bytes_accessed=4 << 20, transcendentals=0),
        name=name,
    )


def partial_half(half, weight, cotangent, dtype):
    planes, _, rows, width = weight.shape
    count = cotangent.shape[0]

    def kernel(half_ref, weight_ref, cotangent_ref, out_ref):
        for plane in range(planes):
            out_ref[plane] = lax.dot_general(
                weight_ref[plane, half_ref[0]],
                cotangent_ref[...],
                LANES,
                preferred_element_type=jnp.float32,
            ).astype(dtype)

    return call(
        kernel,
        [SMEM, VMEM, VMEM],
        jax.ShapeDtypeStruct((planes, rows, count), dtype),
        2 * planes * rows * width * count,
        name="partial_grad_gated",
    )(half, weight, cotangent)


def total_share(share, received):
    def kernel(share_ref, received_ref, out_ref):
        total = share_ref[...] + received_ref[...].astype(jnp.float32)
        out_ref[...] = total.astype(jnp.bfloat16)

    return call(
        kernel,
        [VMEM, VMEM],
        jax.ShapeDtypeStruct(share.shape, jnp.bfloat16),
        1 << 24,
        name="total_share",
    )(share, received)


def project_half(half, gated, weight, before=None):
    planes, rows, width = weight.shape[0], weight.shape[-2], weight.shape[-1]
    count = gated.shape[-1]
    result = jax.ShapeDtypeStruct((count, width), jnp.float32 if before is None else jnp.bfloat16)

    def early(half_ref, gated_ref, weight_ref, out_ref, kept_ref, moved):
        copy = pltpu.make_async_copy(weight_ref.at[:, 1 - half_ref[0]], kept_ref, moved)
        copy.start()
        total = jnp.zeros((count, width), jnp.float32)
        for plane in range(planes):
            total = total + lax.dot_general(
                gated_ref[plane],
                weight_ref[plane, half_ref[0]],
                ROWS,
                preferred_element_type=jnp.float32,
            )
        out_ref[...] = total
        copy.wait()

    def late(gated_ref, weight_ref, before_ref, out_ref):
        total = before_ref[...]
        for plane in range(planes):
            total = total + lax.dot_general(
                gated_ref[plane], weight_ref[plane], ROWS, preferred_element_type=jnp.float32
            )
        out_ref[...] = total.astype(out_ref.dtype)

    flops = 2 * planes * rows * width * count
    if before is None:
        kept = jax.ShapeDtypeStruct((planes, rows, width), weight.dtype)
        return call(
            early,
            [SMEM, VMEM, VMEM],
            [result, kept],
            flops,
            [pltpu.SemaphoreType.DMA],
            name="output_early",
        )(half, gated, weight)
    return call(late, [VMEM] * 3, result, flops, name="output_late")(gated, weight, before)


def first(half, weight, cotangent, projected, filters, seq):
    planes, _, rows, width = weight.shape
    _, channels, count = projected.shape
    per = channels // seq

    def kernel(
        half_ref,
        weight_ref,
        cotangent_ref,
        projected_ref,
        filters_ref,
        share_ref,
        packed_ref,
        weight_here,
        cotangent_here,
        projected_here,
        filters_here,
        arrived,
    ):
        places = [
            (projected_ref, projected_here),
            (filters_ref, filters_here),
            (cotangent_ref, cotangent_here),
        ]
        places += [
            (weight_ref.at[plane, half_ref[0]], weight_here.at[plane]) for plane in range(planes)
        ]
        copies = [
            pltpu.make_async_copy(source, target, arrived.at[i])
            for i, (source, target) in enumerate(places)
        ]
        for copy in copies:
            copy.start()
        copies[0].wait()
        copies[1].wait()
        parts = [projected_here[which].astype(jnp.float32) for which in range(3)]
        parts = [part.reshape(seq, per, count) for part in parts + [filters_here[...]]]
        packed_ref[...] = jnp.concatenate(parts, axis=1).astype(jnp.bfloat16)
        copies[2].wait()
        for plane in range(planes):
            copies[3 + plane].wait()
            share_ref[plane] = lax.dot_general(
                weight_here[plane], cotangent_here[...], LANES, preferred_element_type=jnp.float32
            ).astype(jnp.bfloat16)

    return call(
        kernel,
        [SMEM, HBM, HBM, HBM, HBM],
        [
            jax.ShapeDtypeStruct((planes, rows, count), jnp.bfloat16),
            jax.ShapeDtypeStruct((seq, 4 * per, count), jnp.bfloat16),
        ],
        2 * planes * rows * width * count,
        [
            pltpu.VMEM((planes, rows, width), weight.dtype),
            pltpu.VMEM(cotangent.shape, cotangent.dtype),
            pltpu.VMEM(projected.shape, projected.dtype),
            pltpu.VMEM(filters.shape, filters.dtype),
            pltpu.SemaphoreType.DMA((planes + 3,)),
        ],
        "first_share",
        FIRST_LIMIT,
    )(half, weight, cotangent, projected, filters)


def pack_middle(gated, shares, seq):
    planes, channels, count = shares.shape
    per = channels // seq

    def kernel(gated_ref, shares_ref, out_ref):
        total = shares_ref[0].astype(jnp.float32)
        for plane in range(1, planes):
            total = total + shares_ref[plane].astype(jnp.float32)
        there = gated_ref[...].astype(jnp.float32).reshape(seq, per, count)
        out_ref[...] = jnp.concatenate(
            [there, total.reshape(seq, per, count)], axis=1
        ).astype(jnp.bfloat16)

    return call(
        kernel,
        [VMEM, VMEM],
        jax.ShapeDtypeStruct((seq, 2 * per, count), jnp.bfloat16),
        1 << 24,
        name="pack_middle",
    )(gated, shares)


def spread(middle, planes):
    seq, rows, count = middle.shape
    per = rows // 2

    def kernel(middle_ref, out_ref):
        gated = middle_ref[...].astype(jnp.float32)[:, :per].reshape(seq * per, count)
        gated = gated.astype(jnp.bfloat16)
        for plane in range(planes):
            out_ref[plane] = gated

    return call(
        kernel,
        [VMEM],
        jax.ShapeDtypeStruct((planes, seq * per, count), jnp.bfloat16),
        1 << 24,
        name="spread_gated",
    )(middle)


def unpack(grads, per):
    pairs, rows, count = grads.shape
    seq = 2 * pairs

    def kernel(grads_ref, out_ref):
        there = grads_ref[...].astype(jnp.float32).reshape(seq, 3, per, count)
        for which in range(3):
            out_ref[which] = there[:, which].reshape(seq * per, count).astype(jnp.bfloat16)

    return call(
        kernel,
        [VMEM],
        jax.ShapeDtypeStruct((3, seq * per, count), jnp.bfloat16),
        1 << 24,
        name="unpack_grads",
    )(grads)


def causal(given, skip):
    chunks, rows, _ = given.shape
    per = rows // 4

    def kernel(skip_ref, given_ref, gated_ref, inner_ref, toeplitz_ref, wide, shifted, collected):
        wide[...] = given_ref[...].astype(jnp.float32).reshape(chunks * rows, BLOCK)
        shifted[pl.ds(0, chunks), :] = jnp.zeros((chunks, BLOCK), jnp.float32)
        upper = lax.broadcasted_iota(jnp.int32, (BLOCK, BLOCK), 1) >= lax.broadcasted_iota(
            jnp.int32, (BLOCK, BLOCK), 0
        )

        @pl.loop(0, per)
        def _(channel):
            def take(which):
                return wide[pl.ds(which * per + channel, chunks, stride=rows), :]

            query, mixed, taps = take(0), take(1) * take(2), take(3)
            shifted[pl.ds(chunks, chunks), :] = mixed
            before = jnp.zeros((BLOCK, BLOCK), jnp.float32)
            total = jnp.zeros((chunks, BLOCK), jnp.float32)
            for lag in range(0, chunks, 2):
                blocks, signals = [], []
                for one in (lag, lag + 1):
                    spread = jnp.broadcast_to(taps[one : one + 1, :], (BLOCK, BLOCK))
                    turned = pltpu.roll(spread, 0, 1, stride=1, stride_axis=0)
                    block = jnp.where(upper, turned, before).astype(jnp.bfloat16)
                    before = turned
                    toeplitz_ref[channel, :, one * BLOCK : (one + 1) * BLOCK] = block
                    blocks.append(block)
                    signals.append(shifted[chunks - one : 2 * chunks - one, :].astype(jnp.bfloat16))
                total = total + jnp.dot(
                    jnp.concatenate(signals, axis=1),
                    jnp.concatenate(blocks, axis=0),
                    preferred_element_type=jnp.float32,
                )
            inner = total + skip_ref[channel] * mixed
            inner_ref[channel] = inner
            collected[pl.ds(channel, chunks, stride=per), :] = query * inner

        gated_ref[...] = collected[...].astype(jnp.bfloat16).reshape(gated_ref.shape)

    return call(
        kernel,
        [SMEM, VMEM],
        [
            jax.ShapeDtypeStruct((chunks // 2, 2 * per, BLOCK), jnp.bfloat16),
            jax.ShapeDtypeStruct((per, chunks, BLOCK), jnp.float32),
            jax.ShapeDtypeStruct((per, BLOCK, chunks * BLOCK), jnp.bfloat16),
        ],
        16 * per * chunks * chunks * BLOCK * BLOCK,
        [
            pltpu.VMEM((chunks * rows, BLOCK), jnp.float32),
            pltpu.VMEM((2 * chunks, BLOCK), jnp.float32),
            pltpu.VMEM((chunks * per, BLOCK), jnp.float32),
        ],
        "causal_sum",
    )(skip, given)


def adjoint(given, back, inner, toeplitz, skip):
    chunks, rows, _ = given.shape
    per = rows // 4

    def kernel(
        skip_ref, given_ref, back_ref, inner_ref, toeplitz_ref, out_ref, wide, grads, shifted, collected
    ):
        wide[...] = given_ref[...].astype(jnp.float32).reshape(chunks * rows, BLOCK)
        grads[...] = back_ref[...].astype(jnp.float32).reshape(chunks * 2 * per, BLOCK)
        shifted[pl.ds(chunks, chunks), :] = jnp.zeros((chunks, BLOCK), jnp.float32)

        @pl.loop(0, per)
        def _(channel):
            def take(which):
                return wide[pl.ds(which * per + channel, chunks, stride=rows), :]

            query, key_in, value = take(0), take(1), take(2)
            grad_gated = grads[pl.ds(per + channel, chunks, stride=2 * per), :]
            grad_inner = grad_gated * query
            shifted[pl.ds(0, chunks), :] = grad_inner
            total = jnp.zeros((chunks, BLOCK), jnp.float32)
            for lag in range(0, chunks, 2):
                signals = [shifted[one : one + chunks, :] for one in (lag, lag + 1)]
                total = total + lax.dot_general(
                    jnp.concatenate(signals, axis=1).astype(jnp.bfloat16),
                    toeplitz_ref[channel, :, lag * BLOCK : (lag + 2) * BLOCK],
                    LANES,
                    preferred_element_type=jnp.float32,
                )
            grad_mixed = total + skip_ref[channel] * grad_inner
            results = (grad_gated * inner_ref[channel], grad_mixed * value, grad_mixed * key_in)
            for which, result in enumerate(results):
                collected[pl.ds(which * per + channel, chunks, stride=3 * per), :] = result

        out_ref[...] = collected[...].astype(jnp.bfloat16).reshape(out_ref.shape)

    return call(
        kernel,
        [SMEM, VMEM, VMEM, VMEM, VMEM],
        jax.ShapeDtypeStruct((chunks // 2, 6 * per, BLOCK), jnp.bfloat16),
        16 * per * chunks * chunks * BLOCK * BLOCK,
        [
            pltpu.VMEM((chunks * rows, BLOCK), jnp.float32),
            pltpu.VMEM((chunks * 2 * per, BLOCK), jnp.float32),
            pltpu.VMEM((2 * chunks, BLOCK), jnp.float32),
            pltpu.VMEM((chunks * 3 * per, BLOCK), jnp.float32),
        ],
        "adjoint_sum",
    )(skip, given, back, inner, toeplitz)


def per_device(projected, filters, skip, out_weight, cotangent):
    seq = lax.axis_size("seq")
    chan = lax.axis_size("chan")
    planes = chan // 2
    channels, count = filters.shape
    per = channels // seq
    half = lax.axis_index("chan") & 1
    own, other = half.reshape(1), (1 - half).reshape(1)
    along_z = [[2 * z + h for z in range(planes)] for h in range(2)]
    pairs = [(i, i ^ 1) for i in range(chan)]

    def exchange_seq(array):
        return lax.all_to_all(array, "seq", 0, 0, tiled=True)

    def exchange_z(array):
        return lax.all_to_all(array, "chan", 0, 0, tiled=True, axis_index_groups=along_z)

    weight = out_weight.reshape(planes, 2, channels, out_weight.shape[1])
    share_other, packed = first(other, weight, cotangent, projected, filters, seq)
    received = lax.ppermute(share_other, "chan", pairs)
    given = exchange_seq(packed)
    share_own = partial_half(own, weight, cotangent, jnp.float32)
    skip_here = lax.dynamic_slice(skip, (lax.axis_index("seq") * per,), (per,))
    gated, inner, toeplitz = causal(given, skip_here)
    shares = exchange_z(total_share(share_own, received))
    middle = exchange_seq(pack_middle(gated, shares, seq))
    gated_half = exchange_z(spread(middle, planes))
    grads_there = adjoint(given, middle, inner, toeplitz, skip_here)
    grads_there, gated_half = lax.optimization_barrier((grads_there, gated_half))
    gated_other = lax.ppermute(gated_half, "chan", pairs)
    output, weight_other = project_half(own, gated_half, weight)
    grads = exchange_seq(grads_there.reshape(seq, 3 * per, count))
    output = project_half(other, gated_other, weight_other, output)
    grads, output = lax.optimization_barrier((grads, output))
    grads = unpack(grads.reshape(seq // 2, 6 * per, count), per)
    return output, grads


def solution(mesh):
    in_specs = (
        P(None, "chan", "seq"),
        P("chan", "seq"),
        P("chan"),
        P(None, "chan"),
        P("seq", "chan"),
    )
    out_specs = (P("seq", "chan"), P(None, "chan", "seq"))
    return jax.shard_map(
        per_device, mesh=mesh, in_specs=in_specs, out_specs=out_specs, check_vma=False
    )
```

```python
import jax
import jax.numpy as jnp
from jax import lax
from jax.experimental import pallas as pl
from jax.experimental.pallas import tpu as pltpu
from jax.sharding import PartitionSpec as P

BLOCK = 128
LANES = (((1,), (1,)), ((), ()))
ROWS = (((0,), (0,)), ((), ()))
VMEM_LIMIT = 8 << 20
FIRST_LIMIT = 54 << 20
FIRST_SUM = 7
FIRST_GATED = 5
VMEM = pl.BlockSpec(memory_space=pltpu.VMEM)
HBM = pl.BlockSpec(memory_space=pltpu.HBM)
SMEM = pl.BlockSpec(memory_space=pltpu.SMEM)


def call(kernel, in_specs, out_shape, flops, scratch=(), name=None, limit=VMEM_LIMIT, out=VMEM):
    return pl.pallas_call(
        kernel,
        in_specs=in_specs,
        out_specs=jax.tree.map(lambda _: out, out_shape),
        out_shape=out_shape,
        scratch_shapes=list(scratch),
        compiler_params=pltpu.CompilerParams(vmem_limit_bytes=limit),
        cost_estimate=pl.CostEstimate(flops=flops, bytes_accessed=4 << 20, transcendentals=0),
        name=name,
    )


def partial_half(half, weight, cotangent, dtype):
    planes, _, rows, width = weight.shape
    count = cotangent.shape[0]

    def kernel(half_ref, weight_ref, cotangent_ref, out_ref):
        for plane in range(planes):
            out_ref[plane] = lax.dot_general(
                weight_ref[plane, half_ref[0]],
                cotangent_ref[...],
                LANES,
                preferred_element_type=jnp.float32,
            ).astype(dtype)

    return call(
        kernel,
        [SMEM, VMEM, VMEM],
        jax.ShapeDtypeStruct((planes, rows, count), dtype),
        2 * planes * rows * width * count,
        name="partial_grad_gated",
    )(half, weight, cotangent)


def total_share(share, received, first):
    planes = share.shape[0]

    def kernel(share_ref, received_ref, out_ref):
        for place in range(planes):
            plane = (place + first) % planes
            total = share_ref[plane] + received_ref[plane].astype(jnp.float32)
            out_ref[place] = total.astype(jnp.bfloat16)

    return call(
        kernel,
        [VMEM, VMEM],
        jax.ShapeDtypeStruct(share.shape, jnp.bfloat16),
        1 << 24,
        name="total_share",
    )(share, received)


def project_half(half, gated, weight, first, before=None):
    planes, rows, width = weight.shape[0], weight.shape[-2], weight.shape[-1]
    count = gated.shape[-1]
    result = jax.ShapeDtypeStruct((count, width), jnp.float32 if before is None else jnp.bfloat16)

    def early(half_ref, gated_ref, weight_ref, out_ref, kept_ref, moved):
        copy = pltpu.make_async_copy(weight_ref.at[:, 1 - half_ref[0]], kept_ref, moved)
        copy.start()
        total = jnp.zeros((count, width), jnp.float32)
        for plane in range(planes):
            total = total + lax.dot_general(
                gated_ref[plane],
                weight_ref[(plane + first) % planes, half_ref[0]],
                ROWS,
                preferred_element_type=jnp.float32,
            )
        out_ref[...] = total
        copy.wait()

    def late(gated_ref, weight_ref, before_ref, out_ref):
        total = before_ref[...]
        for plane in range(planes):
            total = total + lax.dot_general(
                gated_ref[plane],
                weight_ref[(plane + first) % planes],
                ROWS,
                preferred_element_type=jnp.float32,
            )
        out_ref[...] = total.astype(out_ref.dtype)

    flops = 2 * planes * rows * width * count
    if before is None:
        kept = jax.ShapeDtypeStruct((planes, rows, width), weight.dtype)
        return call(
            early,
            [SMEM, VMEM, VMEM],
            [result, kept],
            flops,
            [pltpu.SemaphoreType.DMA],
            name="output_early",
        )(half, gated, weight)
    return call(late, [VMEM] * 3, result, flops, name="output_late")(gated, weight, before)


def first(half, weight, cotangent, projected, filters, seq):
    planes, _, rows, width = weight.shape
    _, channels, count = projected.shape
    per = channels // seq

    def kernel(
        half_ref,
        weight_ref,
        cotangent_ref,
        projected_ref,
        filters_ref,
        share_ref,
        packed_ref,
        weight_here,
        cotangent_here,
        projected_here,
        filters_here,
        share_here,
        packed_here,
        arrived,
        left,
    ):
        places = [
            (projected_ref, projected_here),
            (filters_ref, filters_here),
            (cotangent_ref, cotangent_here),
        ]
        places += [
            (weight_ref.at[plane, half_ref[0]], weight_here.at[plane]) for plane in range(planes)
        ]
        copies = [
            pltpu.make_async_copy(source, target, arrived.at[i])
            for i, (source, target) in enumerate(places)
        ]
        for copy in copies:
            copy.start()
        copies[0].wait()
        copies[1].wait()
        parts = [projected_here[which].astype(jnp.float32) for which in range(3)]
        parts = [part.reshape(seq, per, count) for part in parts + [filters_here[...]]]
        packed_here[...] = jnp.concatenate(parts, axis=1).astype(jnp.bfloat16)
        leaving = [pltpu.make_async_copy(packed_here, packed_ref, left.at[planes])]
        leaving[0].start()
        copies[2].wait()
        for plane in range(planes):
            copies[3 + plane].wait()
            share_here[plane] = lax.dot_general(
                weight_here[plane], cotangent_here[...], LANES, preferred_element_type=jnp.float32
            ).astype(jnp.bfloat16)
            leaving.append(
                pltpu.make_async_copy(share_here.at[plane], share_ref.at[plane], left.at[plane])
            )
            leaving[-1].start()
        for copy in leaving:
            copy.wait()

    return call(
        kernel,
        [SMEM, HBM, HBM, HBM, HBM],
        [
            jax.ShapeDtypeStruct((planes, rows, count), jnp.bfloat16),
            jax.ShapeDtypeStruct((seq, 4 * per, count), jnp.bfloat16),
        ],
        2 * planes * rows * width * count,
        [
            pltpu.VMEM((planes, rows, width), weight.dtype),
            pltpu.VMEM(cotangent.shape, cotangent.dtype),
            pltpu.VMEM(projected.shape, projected.dtype),
            pltpu.VMEM(filters.shape, filters.dtype),
            pltpu.VMEM((planes, rows, count), jnp.bfloat16),
            pltpu.VMEM((seq, 4 * per, count), jnp.bfloat16),
            pltpu.SemaphoreType.DMA((planes + 3,)),
            pltpu.SemaphoreType.DMA((planes + 1,)),
        ],
        "first_share",
        FIRST_LIMIT,
        HBM,
    )(half, weight, cotangent, projected, filters)


def pack_middle(gated, shares, seq):
    planes, channels, count = shares.shape
    per = channels // seq

    def kernel(gated_ref, shares_ref, out_ref):
        total = shares_ref[0].astype(jnp.float32)
        for plane in range(1, planes):
            total = total + shares_ref[plane].astype(jnp.float32)
        there = gated_ref[...].astype(jnp.float32).reshape(seq, per, count)
        out_ref[...] = jnp.concatenate(
            [there, total.reshape(seq, per, count)], axis=1
        ).astype(jnp.bfloat16)

    return call(
        kernel,
        [VMEM, VMEM],
        jax.ShapeDtypeStruct((seq, 2 * per, count), jnp.bfloat16),
        1 << 24,
        name="pack_middle",
    )(gated, shares)


def spread(middle, planes):
    seq, rows, count = middle.shape
    per = rows // 2

    def kernel(middle_ref, out_ref, gated, left):
        there = middle_ref[...].astype(jnp.float32)[:, :per].reshape(seq * per, count)
        gated[...] = there.astype(jnp.bfloat16)
        copies = [
            pltpu.make_async_copy(gated, out_ref.at[plane], left.at[plane])
            for plane in range(planes)
        ]
        for copy in copies:
            copy.start()
        for copy in copies:
            copy.wait()

    return call(
        kernel,
        [VMEM],
        jax.ShapeDtypeStruct((planes, seq * per, count), jnp.bfloat16),
        1 << 24,
        [pltpu.VMEM((seq * per, count), jnp.bfloat16), pltpu.SemaphoreType.DMA((planes,))],
        "spread_gated",
        out=HBM,
    )(middle)


def unpack(grads, per):
    pairs, rows, count = grads.shape
    seq = 2 * pairs

    def kernel(grads_ref, out_ref):
        there = grads_ref[...].astype(jnp.float32).reshape(seq, 3, per, count)
        for which in range(3):
            out_ref[which] = there[:, which].reshape(seq * per, count).astype(jnp.bfloat16)

    return call(
        kernel,
        [VMEM],
        jax.ShapeDtypeStruct((3, seq * per, count), jnp.bfloat16),
        1 << 24,
        name="unpack_grads",
    )(grads)


def turn(rows):
    middle = rows.shape[0] // 2
    return jnp.concatenate([rows[middle:], rows[:middle]], axis=0)


def causal(given, skip):
    chunks, rows, _ = given.shape
    per = rows // 4

    def kernel(skip_ref, given_ref, gated_ref, inner_ref, toeplitz_ref, wide, shifted, collected):
        wide[...] = given_ref[...].astype(jnp.float32).reshape(chunks * rows, BLOCK)
        shifted[pl.ds(0, chunks), :] = jnp.zeros((chunks, BLOCK), jnp.float32)
        upper = lax.broadcasted_iota(jnp.int32, (BLOCK, BLOCK), 1) >= lax.broadcasted_iota(
            jnp.int32, (BLOCK, BLOCK), 0
        )

        @pl.loop(0, per)
        def _(channel):
            def take(which):
                return turn(wide[pl.ds(which * per + channel, chunks, stride=rows), :])

            query, mixed, taps = take(0), take(1) * take(2), take(3)
            shifted[pl.ds(chunks, chunks), :] = mixed
            before = jnp.zeros((BLOCK, BLOCK), jnp.float32)
            total = jnp.zeros((chunks, BLOCK), jnp.float32)
            for lag in range(0, chunks, 2):
                blocks, signals = [], []
                for one in (lag, lag + 1):
                    spread = jnp.broadcast_to(taps[one : one + 1, :], (BLOCK, BLOCK))
                    turned = pltpu.roll(spread, 0, 1, stride=1, stride_axis=0)
                    block = jnp.where(upper, turned, before).astype(jnp.bfloat16)
                    before = turned
                    toeplitz_ref[channel, :, one * BLOCK : (one + 1) * BLOCK] = block
                    blocks.append(block)
                    signals.append(shifted[chunks - one : 2 * chunks - one, :].astype(jnp.bfloat16))
                total = total + jnp.dot(
                    jnp.concatenate(signals, axis=1),
                    jnp.concatenate(blocks, axis=0),
                    preferred_element_type=jnp.float32,
                )
            inner = total + skip_ref[channel] * mixed
            inner_ref[channel] = inner
            collected[pl.ds(channel, chunks, stride=per), :] = turn(query * inner)

        gated_ref[...] = collected[...].astype(jnp.bfloat16).reshape(gated_ref.shape)

    return call(
        kernel,
        [SMEM, VMEM],
        [
            jax.ShapeDtypeStruct((chunks // 2, 2 * per, BLOCK), jnp.bfloat16),
            jax.ShapeDtypeStruct((per, chunks, BLOCK), jnp.float32),
            jax.ShapeDtypeStruct((per, BLOCK, chunks * BLOCK), jnp.bfloat16),
        ],
        16 * per * chunks * chunks * BLOCK * BLOCK,
        [
            pltpu.VMEM((chunks * rows, BLOCK), jnp.float32),
            pltpu.VMEM((2 * chunks, BLOCK), jnp.float32),
            pltpu.VMEM((chunks * per, BLOCK), jnp.float32),
        ],
        "causal_sum",
    )(skip, given)


def adjoint(given, back, inner, toeplitz, skip):
    chunks, rows, _ = given.shape
    per = rows // 4

    def kernel(
        skip_ref, given_ref, back_ref, inner_ref, toeplitz_ref, out_ref, wide, grads, shifted, collected
    ):
        wide[...] = given_ref[...].astype(jnp.float32).reshape(chunks * rows, BLOCK)
        grads[...] = back_ref[...].astype(jnp.float32).reshape(chunks * 2 * per, BLOCK)
        shifted[pl.ds(chunks, chunks), :] = jnp.zeros((chunks, BLOCK), jnp.float32)

        @pl.loop(0, per)
        def _(channel):
            def take(which):
                return turn(wide[pl.ds(which * per + channel, chunks, stride=rows), :])

            query, key_in, value = take(0), take(1), take(2)
            grad_gated = turn(grads[pl.ds(per + channel, chunks, stride=2 * per), :])
            grad_inner = grad_gated * query
            shifted[pl.ds(0, chunks), :] = grad_inner
            total = jnp.zeros((chunks, BLOCK), jnp.float32)
            for lag in range(0, chunks, 2):
                signals = [shifted[one : one + chunks, :] for one in (lag, lag + 1)]
                total = total + lax.dot_general(
                    jnp.concatenate(signals, axis=1).astype(jnp.bfloat16),
                    toeplitz_ref[channel, :, lag * BLOCK : (lag + 2) * BLOCK],
                    LANES,
                    preferred_element_type=jnp.float32,
                )
            grad_mixed = total + skip_ref[channel] * grad_inner
            results = (grad_gated * inner_ref[channel], grad_mixed * value, grad_mixed * key_in)
            for which, result in enumerate(results):
                collected[pl.ds(which * per + channel, chunks, stride=3 * per), :] = turn(result)

        out_ref[...] = collected[...].astype(jnp.bfloat16).reshape(out_ref.shape)

    return call(
        kernel,
        [SMEM, VMEM, VMEM, VMEM, VMEM],
        jax.ShapeDtypeStruct((chunks // 2, 6 * per, BLOCK), jnp.bfloat16),
        16 * per * chunks * chunks * BLOCK * BLOCK,
        [
            pltpu.VMEM((chunks * rows, BLOCK), jnp.float32),
            pltpu.VMEM((chunks * 2 * per, BLOCK), jnp.float32),
            pltpu.VMEM((2 * chunks, BLOCK), jnp.float32),
            pltpu.VMEM((chunks * 3 * per, BLOCK), jnp.float32),
        ],
        "adjoint_sum",
    )(skip, given, back, inner, toeplitz)


def per_device(projected, filters, skip, out_weight, cotangent):
    seq = lax.axis_size("seq")
    chan = lax.axis_size("chan")
    planes = chan // 2
    channels, count = filters.shape
    per = channels // seq
    half = lax.axis_index("chan") & 1
    own, other = half.reshape(1), (1 - half).reshape(1)
    along_z = [[2 * z + h for z in range(planes)] for h in range(2)]
    pairs = [(i, i ^ 1) for i in range(chan)]

    along_seq = [[(place + seq // 2) % seq for place in range(seq)]]

    def exchange_seq(array):
        return lax.all_to_all(array, "seq", 0, 0, tiled=True, axis_index_groups=along_seq)

    def exchange_z(array, first=0):
        groups = [group[first:] + group[:first] for group in along_z]
        return lax.all_to_all(array, "chan", 0, 0, tiled=True, axis_index_groups=groups)

    weight = out_weight.reshape(planes, 2, channels, out_weight.shape[1])
    share_other, packed = first(other, weight, cotangent, projected, filters, seq)
    received = lax.ppermute(share_other, "chan", pairs)
    given = exchange_seq(packed)
    share_own = partial_half(own, weight, cotangent, jnp.float32)
    skip_here = lax.dynamic_slice(skip, ((lax.axis_index("seq") + seq // 2) % seq * per,), (per,))
    gated, inner, toeplitz = causal(given, skip_here)
    shares = exchange_z(total_share(share_own, received, FIRST_SUM), FIRST_SUM)
    middle = exchange_seq(pack_middle(gated, shares, seq))
    gated_half = exchange_z(spread(middle, planes), FIRST_GATED)
    grads_there = adjoint(given, middle, inner, toeplitz, skip_here)
    grads_there, gated_half = lax.optimization_barrier((grads_there, gated_half))
    gated_other = lax.ppermute(gated_half, "chan", pairs)
    output, weight_other = project_half(own, gated_half, weight, FIRST_GATED)
    grads = exchange_seq(grads_there.reshape(seq, 3 * per, count))
    output = project_half(other, gated_other, weight_other, FIRST_GATED, output)
    grads, output = lax.optimization_barrier((grads, output))
    grads = unpack(grads.reshape(seq // 2, 6 * per, count), per)
    return output, grads


def solution(mesh):
    in_specs = (
        P(None, "chan", "seq"),
        P("chan", "seq"),
        P("chan"),
        P(None, "chan"),
        P("seq", "chan"),
    )
    out_specs = (P("seq", "chan"), P(None, "chan", "seq"))
    return jax.shard_map(
        per_device, mesh=mesh, in_specs=in_specs, out_specs=out_specs, check_vma=False
    )
```

```python
import jax
import jax.numpy as jnp
from jax import lax
from jax.experimental import pallas as pl
from jax.experimental.pallas import tpu as pltpu
from jax.sharding import PartitionSpec as P

BLOCK = 128
LANES = (((1,), (1,)), ((), ()))
ROWS = (((0,), (0,)), ((), ()))
VMEM_LIMIT = 8 << 20
FIRST_LIMIT = 54 << 20
FIRST_SUM = 7
FIRST_GATED = 5
FIRST_GIVEN = 18
FIRST_MIDDLE = 18
FIRST_BACK = 18
VMEM = pl.BlockSpec(memory_space=pltpu.VMEM)
HBM = pl.BlockSpec(memory_space=pltpu.HBM)
SMEM = pl.BlockSpec(memory_space=pltpu.SMEM)


def call(kernel, in_specs, out_shape, flops, scratch=(), name=None, limit=VMEM_LIMIT, out=VMEM):
    return pl.pallas_call(
        kernel,
        in_specs=in_specs,
        out_specs=jax.tree.map(lambda _: out, out_shape),
        out_shape=out_shape,
        scratch_shapes=list(scratch),
        compiler_params=pltpu.CompilerParams(vmem_limit_bytes=limit),
        cost_estimate=pl.CostEstimate(flops=flops, bytes_accessed=4 << 20, transcendentals=0),
        name=name,
    )


def partial_half(half, weight, cotangent, dtype):
    planes, _, rows, width = weight.shape
    count = cotangent.shape[0]

    def kernel(half_ref, weight_ref, cotangent_ref, out_ref):
        for plane in range(planes):
            out_ref[plane] = lax.dot_general(
                weight_ref[plane, half_ref[0]],
                cotangent_ref[...],
                LANES,
                preferred_element_type=jnp.float32,
            ).astype(dtype)

    return call(
        kernel,
        [SMEM, VMEM, VMEM],
        jax.ShapeDtypeStruct((planes, rows, count), dtype),
        2 * planes * rows * width * count,
        name="partial_grad_gated",
    )(half, weight, cotangent)


def total_share(share, received, first):
    planes = share.shape[0]

    def kernel(share_ref, received_ref, out_ref):
        for place in range(planes):
            plane = (place + first) % planes
            total = share_ref[plane] + received_ref[plane].astype(jnp.float32)
            out_ref[place] = total.astype(jnp.bfloat16)

    return call(
        kernel,
        [VMEM, VMEM],
        jax.ShapeDtypeStruct(share.shape, jnp.bfloat16),
        1 << 24,
        name="total_share",
    )(share, received)


def project_half(half, gated, weight, first, before=None):
    planes, rows, width = weight.shape[0], weight.shape[-2], weight.shape[-1]
    count = gated.shape[-1]
    result = jax.ShapeDtypeStruct((count, width), jnp.float32 if before is None else jnp.bfloat16)

    def early(half_ref, gated_ref, weight_ref, out_ref, kept_ref, moved):
        copies = [
            pltpu.make_async_copy(
                weight_ref.at[(plane + first) % planes, 1 - half_ref[0]],
                kept_ref.at[plane],
                moved.at[plane],
            )
            for plane in range(planes)
        ]
        for copy in copies:
            copy.start()
        total = jnp.zeros((count, width), jnp.float32)
        for plane in range(planes):
            total = total + lax.dot_general(
                gated_ref[plane],
                weight_ref[(plane + first) % planes, half_ref[0]],
                ROWS,
                preferred_element_type=jnp.float32,
            )
        out_ref[...] = total
        for copy in copies:
            copy.wait()

    def late(gated_ref, weight_ref, before_ref, out_ref):
        total = before_ref[...] + lax.dot_general(
            gated_ref[...].reshape(planes * rows, count),
            weight_ref[...].reshape(planes * rows, width),
            ROWS,
            preferred_element_type=jnp.float32,
        )
        out_ref[...] = total.astype(out_ref.dtype)

    flops = 2 * planes * rows * width * count
    if before is None:
        kept = jax.ShapeDtypeStruct((planes, rows, width), weight.dtype)
        return call(
            early,
            [SMEM, VMEM, VMEM],
            [result, kept],
            flops,
            [pltpu.SemaphoreType.DMA((planes,))],
            name="output_early",
        )(half, gated, weight)
    return call(late, [VMEM] * 3, result, flops, name="output_late")(gated, weight, before)


def first(half, weight, cotangent, projected, filters, seq):
    planes, _, rows, width = weight.shape
    _, channels, count = projected.shape
    per = channels // seq

    def kernel(
        half_ref,
        weight_ref,
        cotangent_ref,
        projected_ref,
        filters_ref,
        share_ref,
        packed_ref,
        weight_here,
        cotangent_here,
        projected_here,
        filters_here,
        share_here,
        packed_here,
        arrived,
        left,
    ):
        places = [
            (projected_ref, projected_here),
            (filters_ref, filters_here),
            (cotangent_ref, cotangent_here),
        ]
        group = planes // 2
        places += [
            (weight_ref.at[pl.ds(start, group), half_ref[0]], weight_here.at[pl.ds(start, group)])
            for start in (0, group)
        ]
        copies = [
            pltpu.make_async_copy(source, target, arrived.at[i])
            for i, (source, target) in enumerate(places)
        ]
        for copy in copies:
            copy.start()
        copies[0].wait()
        copies[1].wait()
        parts = [projected_here[which].astype(jnp.float32) for which in range(3)]
        parts = [part.reshape(seq, per, count) for part in parts + [filters_here[...]]]
        packed_here[...] = jnp.concatenate(parts, axis=1).astype(jnp.bfloat16)
        leaving = [pltpu.make_async_copy(packed_here, packed_ref, left.at[2])]
        leaving[0].start()
        copies[2].wait()
        for place, start in enumerate((0, group)):
            copies[3 + place].wait()
            share = lax.dot_general(
                weight_here[pl.ds(start, group)].reshape(group * rows, width),
                cotangent_here[...],
                LANES,
                preferred_element_type=jnp.float32,
            )
            share_here[pl.ds(start, group)] = share.astype(jnp.bfloat16).reshape(group, rows, count)
            leaving.append(
                pltpu.make_async_copy(
                    share_here.at[pl.ds(start, group)],
                    share_ref.at[pl.ds(start, group)],
                    left.at[place],
                )
            )
            leaving[-1].start()
        for copy in leaving:
            copy.wait()

    return call(
        kernel,
        [SMEM, HBM, HBM, HBM, HBM],
        [
            jax.ShapeDtypeStruct((planes, rows, count), jnp.bfloat16),
            jax.ShapeDtypeStruct((seq, 4 * per, count), jnp.bfloat16),
        ],
        2 * planes * rows * width * count,
        [
            pltpu.VMEM((planes, rows, width), weight.dtype),
            pltpu.VMEM(cotangent.shape, cotangent.dtype),
            pltpu.VMEM(projected.shape, projected.dtype),
            pltpu.VMEM(filters.shape, filters.dtype),
            pltpu.VMEM((planes, rows, count), jnp.bfloat16),
            pltpu.VMEM((seq, 4 * per, count), jnp.bfloat16),
            pltpu.SemaphoreType.DMA((5,)),
            pltpu.SemaphoreType.DMA((3,)),
        ],
        "first_share",
        FIRST_LIMIT,
        HBM,
    )(half, weight, cotangent, projected, filters)


def pack_middle(gated, shares, seq):
    planes, channels, count = shares.shape
    per = channels // seq

    def kernel(gated_ref, shares_ref, out_ref):
        total = shares_ref[0].astype(jnp.float32)
        for plane in range(1, planes):
            total = total + shares_ref[plane].astype(jnp.float32)
        there = gated_ref[...].astype(jnp.float32).reshape(seq, per, count)
        out_ref[...] = jnp.concatenate(
            [there, turn(total.reshape(seq, per, count), FIRST_MIDDLE - FIRST_GIVEN)], axis=1
        ).astype(jnp.bfloat16)

    return call(
        kernel,
        [VMEM, VMEM],
        jax.ShapeDtypeStruct((seq, 2 * per, count), jnp.bfloat16),
        1 << 24,
        name="pack_middle",
    )(gated, shares)


def spread(middle, planes):
    seq, rows, count = middle.shape
    per = rows // 2

    def kernel(middle_ref, out_ref, gated, left):
        there = turn(middle_ref[...].astype(jnp.float32)[:, :per], FIRST_GIVEN - FIRST_MIDDLE)
        gated[...] = there.reshape(seq * per, count).astype(jnp.bfloat16)
        copies = [
            pltpu.make_async_copy(gated, out_ref.at[plane], left.at[plane])
            for plane in range(planes)
        ]
        for copy in copies:
            copy.start()
        for copy in copies:
            copy.wait()

    return call(
        kernel,
        [VMEM],
        jax.ShapeDtypeStruct((planes, seq * per, count), jnp.bfloat16),
        1 << 24,
        [pltpu.VMEM((seq * per, count), jnp.bfloat16), pltpu.SemaphoreType.DMA((planes,))],
        "spread_gated",
        out=HBM,
    )(middle)


def unpack(grads, per):
    pairs, rows, count = grads.shape
    seq = 2 * pairs

    def kernel(grads_ref, out_ref):
        there = grads_ref[...].astype(jnp.float32).reshape(seq, 3, per, count)
        there = turn(there, FIRST_GIVEN - FIRST_BACK)
        for which in range(3):
            out_ref[which] = there[:, which].reshape(seq * per, count).astype(jnp.bfloat16)

    return call(
        kernel,
        [VMEM],
        jax.ShapeDtypeStruct((3, seq * per, count), jnp.bfloat16),
        1 << 24,
        name="unpack_grads",
    )(grads)


def turn(array, by):
    by = by % array.shape[0]
    return array if by == 0 else jnp.concatenate([array[by:], array[:by]], axis=0)


def causal(given, skip):
    chunks, rows, _ = given.shape
    per = rows // 4

    def kernel(skip_ref, given_ref, gated_ref, inner_ref, toeplitz_ref, wide, shifted, collected):
        wide[...] = given_ref[...].astype(jnp.float32).reshape(chunks * rows, BLOCK)
        shifted[pl.ds(0, chunks), :] = jnp.zeros((chunks, BLOCK), jnp.float32)
        upper = lax.broadcasted_iota(jnp.int32, (BLOCK, BLOCK), 1) >= lax.broadcasted_iota(
            jnp.int32, (BLOCK, BLOCK), 0
        )

        @pl.loop(0, per)
        def _(channel):
            def take(which):
                return turn(wide[pl.ds(which * per + channel, chunks, stride=rows), :], -FIRST_GIVEN)

            query, mixed, taps = take(0), take(1) * take(2), take(3)
            shifted[pl.ds(chunks, chunks), :] = mixed
            before = jnp.zeros((BLOCK, BLOCK), jnp.float32)
            total = jnp.zeros((chunks, BLOCK), jnp.float32)
            for lag in range(0, chunks, 2):
                blocks, signals = [], []
                for one in (lag, lag + 1):
                    spread = jnp.broadcast_to(taps[one : one + 1, :], (BLOCK, BLOCK))
                    turned = pltpu.roll(spread, 0, 1, stride=1, stride_axis=0)
                    block = jnp.where(upper, turned, before).astype(jnp.bfloat16)
                    before = turned
                    toeplitz_ref[channel, :, one * BLOCK : (one + 1) * BLOCK] = block
                    blocks.append(block)
                    signals.append(shifted[chunks - one : 2 * chunks - one, :].astype(jnp.bfloat16))
                total = total + jnp.dot(
                    jnp.concatenate(signals, axis=1),
                    jnp.concatenate(blocks, axis=0),
                    preferred_element_type=jnp.float32,
                )
            inner = total + skip_ref[channel] * mixed
            inner_ref[channel] = inner
            collected[pl.ds(channel, chunks, stride=per), :] = turn(
                query * inner, FIRST_MIDDLE
            )

        gated_ref[...] = collected[...].astype(jnp.bfloat16).reshape(gated_ref.shape)

    return call(
        kernel,
        [SMEM, VMEM],
        [
            jax.ShapeDtypeStruct((chunks // 2, 2 * per, BLOCK), jnp.bfloat16),
            jax.ShapeDtypeStruct((per, chunks, BLOCK), jnp.float32),
            jax.ShapeDtypeStruct((per, BLOCK, chunks * BLOCK), jnp.bfloat16),
        ],
        16 * per * chunks * chunks * BLOCK * BLOCK,
        [
            pltpu.VMEM((chunks * rows, BLOCK), jnp.float32),
            pltpu.VMEM((2 * chunks, BLOCK), jnp.float32),
            pltpu.VMEM((chunks * per, BLOCK), jnp.float32),
        ],
        "causal_sum",
    )(skip, given)


def adjoint(given, back, inner, toeplitz, skip):
    chunks, rows, _ = given.shape
    per = rows // 4

    def kernel(
        skip_ref, given_ref, back_ref, inner_ref, toeplitz_ref, out_ref, wide, grads, shifted, collected
    ):
        wide[...] = given_ref[...].astype(jnp.float32).reshape(chunks * rows, BLOCK)
        grads[...] = back_ref[...].astype(jnp.float32).reshape(chunks * 2 * per, BLOCK)
        shifted[pl.ds(chunks, chunks), :] = jnp.zeros((chunks, BLOCK), jnp.float32)

        @pl.loop(0, per)
        def _(channel):
            def take(which):
                return turn(wide[pl.ds(which * per + channel, chunks, stride=rows), :], -FIRST_GIVEN)

            query, key_in, value = take(0), take(1), take(2)
            grad_gated = turn(grads[pl.ds(per + channel, chunks, stride=2 * per), :], -FIRST_MIDDLE)
            grad_inner = grad_gated * query
            shifted[pl.ds(0, chunks), :] = grad_inner
            total = jnp.zeros((chunks, BLOCK), jnp.float32)
            for lag in range(0, chunks, 2):
                signals = [shifted[one : one + chunks, :] for one in (lag, lag + 1)]
                total = total + lax.dot_general(
                    jnp.concatenate(signals, axis=1).astype(jnp.bfloat16),
                    toeplitz_ref[channel, :, lag * BLOCK : (lag + 2) * BLOCK],
                    LANES,
                    preferred_element_type=jnp.float32,
                )
            grad_mixed = total + skip_ref[channel] * grad_inner
            results = (grad_gated * inner_ref[channel], grad_mixed * value, grad_mixed * key_in)
            for which, result in enumerate(results):
                collected[pl.ds(which * per + channel, chunks, stride=3 * per), :] = turn(
                    result, FIRST_BACK
                )

        out_ref[...] = collected[...].astype(jnp.bfloat16).reshape(out_ref.shape)

    return call(
        kernel,
        [SMEM, VMEM, VMEM, VMEM, VMEM],
        jax.ShapeDtypeStruct((chunks // 2, 6 * per, BLOCK), jnp.bfloat16),
        16 * per * chunks * chunks * BLOCK * BLOCK,
        [
            pltpu.VMEM((chunks * rows, BLOCK), jnp.float32),
            pltpu.VMEM((chunks * 2 * per, BLOCK), jnp.float32),
            pltpu.VMEM((2 * chunks, BLOCK), jnp.float32),
            pltpu.VMEM((chunks * 3 * per, BLOCK), jnp.float32),
        ],
        "adjoint_sum",
    )(skip, given, back, inner, toeplitz)


def per_device(projected, filters, skip, out_weight, cotangent):
    seq = lax.axis_size("seq")
    chan = lax.axis_size("chan")
    planes = chan // 2
    channels, count = filters.shape
    per = channels // seq
    half = lax.axis_index("chan") & 1
    own, other = half.reshape(1), (1 - half).reshape(1)
    along_z = [[2 * z + h for z in range(planes)] for h in range(2)]
    pairs = [(i, i ^ 1) for i in range(chan)]

    def exchange_seq(array, first):
        groups = [[(place + first) % seq for place in range(seq)]]
        return lax.all_to_all(array, "seq", 0, 0, tiled=True, axis_index_groups=groups)

    def exchange_z(array, first=0):
        groups = [group[first:] + group[:first] for group in along_z]
        return lax.all_to_all(array, "chan", 0, 0, tiled=True, axis_index_groups=groups)

    weight = out_weight.reshape(planes, 2, channels, out_weight.shape[1])
    share_other, packed = first(other, weight, cotangent, projected, filters, seq)
    received = lax.ppermute(share_other, "chan", pairs)
    given = exchange_seq(packed, FIRST_GIVEN)
    share_own = partial_half(own, weight, cotangent, jnp.float32)
    skip_here = lax.dynamic_slice(skip, ((lax.axis_index("seq") - FIRST_GIVEN) % seq * per,), (per,))
    gated, inner, toeplitz = causal(given, skip_here)
    shares = exchange_z(total_share(share_own, received, FIRST_SUM), FIRST_SUM)
    middle = exchange_seq(pack_middle(gated, shares, seq), FIRST_MIDDLE)
    gated_half = exchange_z(spread(middle, planes), FIRST_GATED)
    grads_there = adjoint(given, middle, inner, toeplitz, skip_here)
    grads_there, gated_half = lax.optimization_barrier((grads_there, gated_half))
    gated_other = lax.ppermute(gated_half, "chan", pairs)
    output, weight_other = project_half(own, gated_half, weight, FIRST_GATED)
    grads = exchange_seq(grads_there.reshape(seq, 3 * per, count), FIRST_BACK)
    output = project_half(other, gated_other, weight_other, FIRST_GATED, output)
    grads, output = lax.optimization_barrier((grads, output))
    grads = unpack(grads.reshape(seq // 2, 6 * per, count), per)
    return output, grads


def solution(mesh):
    in_specs = (
        P(None, "chan", "seq"),
        P("chan", "seq"),
        P("chan"),
        P(None, "chan"),
        P("seq", "chan"),
    )
    out_specs = (P("seq", "chan"), P(None, "chan", "seq"))
    return jax.shard_map(
        per_device, mesh=mesh, in_specs=in_specs, out_specs=out_specs, check_vma=False
    )
```

```python
import jax
import jax.numpy as jnp
from jax import lax
from jax.experimental import pallas as pl
from jax.experimental.pallas import tpu as pltpu
from jax.sharding import PartitionSpec as P

BLOCK = 128
LANES = (((1,), (1,)), ((), ()))
ROWS = (((0,), (0,)), ((), ()))
VMEM_LIMIT = 8 << 20
FIRST_LIMIT = 54 << 20
FIRST_SUM = 7
FIRST_GATED = 5
FIRST_SEQ = 18
VMEM = pl.BlockSpec(memory_space=pltpu.VMEM)
HBM = pl.BlockSpec(memory_space=pltpu.HBM)
SMEM = pl.BlockSpec(memory_space=pltpu.SMEM)


def call(kernel, in_specs, out_shape, flops, scratch=(), name=None, limit=VMEM_LIMIT, out=VMEM):
    return pl.pallas_call(
        kernel,
        in_specs=in_specs,
        out_specs=jax.tree.map(lambda _: out, out_shape),
        out_shape=out_shape,
        scratch_shapes=list(scratch),
        compiler_params=pltpu.CompilerParams(vmem_limit_bytes=limit),
        cost_estimate=pl.CostEstimate(flops=flops, bytes_accessed=4 << 20, transcendentals=0),
        name=name,
    )


def partial_half(half, weight, cotangent, dtype):
    planes, _, rows, width = weight.shape
    count = cotangent.shape[0]

    def kernel(half_ref, weight_ref, cotangent_ref, out_ref):
        for plane in range(planes):
            out_ref[plane] = lax.dot_general(
                weight_ref[plane, half_ref[0]],
                cotangent_ref[...],
                LANES,
                preferred_element_type=jnp.float32,
            ).astype(dtype)

    return call(
        kernel,
        [SMEM, VMEM, VMEM],
        jax.ShapeDtypeStruct((planes, rows, count), dtype),
        2 * planes * rows * width * count,
        name="partial_grad_gated",
    )(half, weight, cotangent)


def total_share(share, received, first):
    planes = share.shape[0]

    def kernel(share_ref, received_ref, out_ref):
        for place in range(planes):
            plane = (place + first) % planes
            total = share_ref[plane] + received_ref[plane].astype(jnp.float32)
            out_ref[place] = total.astype(jnp.bfloat16)

    return call(
        kernel,
        [VMEM, VMEM],
        jax.ShapeDtypeStruct(share.shape, jnp.bfloat16),
        1 << 24,
        name="total_share",
    )(share, received)


def project_half(half, gated, weight, first, before=None):
    planes, rows, width = weight.shape[0], weight.shape[-2], weight.shape[-1]
    count = gated.shape[-1]
    result = jax.ShapeDtypeStruct((count, width), jnp.float32 if before is None else jnp.bfloat16)

    def early(half_ref, gated_ref, weight_ref, out_ref, kept_ref, moved):
        copies = [
            pltpu.make_async_copy(
                weight_ref.at[(plane + first) % planes, 1 - half_ref[0]],
                kept_ref.at[plane],
                moved.at[plane],
            )
            for plane in range(planes)
        ]
        for copy in copies:
            copy.start()
        total = jnp.zeros((count, width), jnp.float32)
        for plane in range(planes):
            total = total + lax.dot_general(
                gated_ref[plane],
                weight_ref[(plane + first) % planes, half_ref[0]],
                ROWS,
                preferred_element_type=jnp.float32,
            )
        out_ref[...] = total
        for copy in copies:
            copy.wait()

    def late(gated_ref, weight_ref, before_ref, out_ref):
        total = before_ref[...] + lax.dot_general(
            gated_ref[...].reshape(planes * rows, count),
            weight_ref[...].reshape(planes * rows, width),
            ROWS,
            preferred_element_type=jnp.float32,
        )
        out_ref[...] = total.astype(out_ref.dtype)

    flops = 2 * planes * rows * width * count
    if before is None:
        kept = jax.ShapeDtypeStruct((planes, rows, width), weight.dtype)
        return call(
            early,
            [SMEM, VMEM, VMEM],
            [result, kept],
            flops,
            [pltpu.SemaphoreType.DMA((planes,))],
            name="output_early",
        )(half, gated, weight)
    return call(late, [VMEM] * 3, result, flops, name="output_late")(gated, weight, before)


def first(half, weight, cotangent, projected, filters, seq):
    planes, _, rows, width = weight.shape
    _, channels, count = projected.shape
    per = channels // seq

    def kernel(
        half_ref,
        weight_ref,
        cotangent_ref,
        projected_ref,
        filters_ref,
        share_ref,
        packed_ref,
        weight_here,
        cotangent_here,
        projected_here,
        filters_here,
        share_here,
        packed_here,
        arrived,
        left,
    ):
        places = [
            (projected_ref.at[pl.ds(1, 2)], projected_here),
            (filters_ref, filters_here),
            (cotangent_ref, cotangent_here),
        ]
        group = planes // 2
        places += [
            (weight_ref.at[pl.ds(start, group), half_ref[0]], weight_here.at[pl.ds(start, group)])
            for start in (0, group)
        ]
        copies = [
            pltpu.make_async_copy(source, target, arrived.at[i])
            for i, (source, target) in enumerate(places)
        ]
        for copy in copies:
            copy.start()
        copies[0].wait()
        copies[1].wait()
        parts = [projected_here[which].astype(jnp.float32) for which in range(2)]
        parts = [part.reshape(seq, per, count) for part in parts + [filters_here[...]]]
        packed_here[...] = jnp.concatenate(parts, axis=1).astype(jnp.bfloat16)
        leaving = [pltpu.make_async_copy(packed_here, packed_ref, left.at[2])]
        leaving[0].start()
        copies[2].wait()
        for place, start in enumerate((0, group)):
            copies[3 + place].wait()
            share = lax.dot_general(
                weight_here[pl.ds(start, group)].reshape(group * rows, width),
                cotangent_here[...],
                LANES,
                preferred_element_type=jnp.float32,
            )
            share_here[pl.ds(start, group)] = share.astype(jnp.bfloat16).reshape(group, rows, count)
            leaving.append(
                pltpu.make_async_copy(
                    share_here.at[pl.ds(start, group)],
                    share_ref.at[pl.ds(start, group)],
                    left.at[place],
                )
            )
            leaving[-1].start()
        for copy in leaving:
            copy.wait()

    return call(
        kernel,
        [SMEM, HBM, HBM, HBM, HBM],
        [
            jax.ShapeDtypeStruct((planes, rows, count), jnp.bfloat16),
            jax.ShapeDtypeStruct((seq, 3 * per, count), jnp.bfloat16),
        ],
        2 * planes * rows * width * count,
        [
            pltpu.VMEM((planes, rows, width), weight.dtype),
            pltpu.VMEM(cotangent.shape, cotangent.dtype),
            pltpu.VMEM((2, channels, count), projected.dtype),
            pltpu.VMEM(filters.shape, filters.dtype),
            pltpu.VMEM((planes, rows, count), jnp.bfloat16),
            pltpu.VMEM((seq, 3 * per, count), jnp.bfloat16),
            pltpu.SemaphoreType.DMA((5,)),
            pltpu.SemaphoreType.DMA((3,)),
        ],
        "first_share",
        FIRST_LIMIT,
        HBM,
    )(half, weight, cotangent, projected, filters)


def pack_middle(inner, shares, projected, seq):
    planes, channels, count = shares.shape
    per = channels // seq

    def kernel(inner_ref, shares_ref, projected_ref, out_ref, total_ref):
        total = shares_ref[0].astype(jnp.float32)
        for plane in range(1, planes):
            total = total + shares_ref[plane].astype(jnp.float32)
        total_ref[...] = total
        back = (total * projected_ref[0].astype(jnp.float32)).reshape(seq, per, count)
        there = inner_ref[...].astype(jnp.float32).reshape(seq, per, count)
        out_ref[...] = jnp.concatenate([there, back], axis=1).astype(jnp.bfloat16)

    return call(
        kernel,
        [VMEM, VMEM, VMEM],
        [
            jax.ShapeDtypeStruct((seq, 2 * per, count), jnp.bfloat16),
            jax.ShapeDtypeStruct((channels, count), jnp.float32),
        ],
        1 << 24,
        name="pack_middle",
    )(inner, shares, projected)


def spread(middle, projected, planes):
    seq, rows, count = middle.shape
    per = rows // 2

    def kernel(middle_ref, projected_ref, out_ref, gated, left):
        inner = middle_ref[...].astype(jnp.float32)[:, :per].reshape(seq * per, count)
        gated[...] = (projected_ref[0].astype(jnp.float32) * inner).astype(jnp.bfloat16)
        copies = [
            pltpu.make_async_copy(gated, out_ref.at[plane], left.at[plane])
            for plane in range(planes)
        ]
        for copy in copies:
            copy.start()
        for copy in copies:
            copy.wait()

    return call(
        kernel,
        [VMEM, VMEM],
        jax.ShapeDtypeStruct((planes, seq * per, count), jnp.bfloat16),
        1 << 24,
        [pltpu.VMEM((seq * per, count), jnp.bfloat16), pltpu.SemaphoreType.DMA((planes,))],
        "spread_gated",
        out=HBM,
    )(middle, projected)


def last_grads(grad_mixed, middle, grad_gated, projected):
    seq, rows, count = middle.shape
    per = rows // 2

    def kernel(grad_mixed_ref, middle_ref, grad_gated_ref, projected_ref, out_ref):
        inner = middle_ref[...].astype(jnp.float32)[:, :per].reshape(seq * per, count)
        mixed = grad_mixed_ref[...].astype(jnp.float32).reshape(seq * per, count)
        out_ref[0] = (grad_gated_ref[...] * inner).astype(jnp.bfloat16)
        out_ref[1] = (mixed * projected_ref[2].astype(jnp.float32)).astype(jnp.bfloat16)
        out_ref[2] = (mixed * projected_ref[1].astype(jnp.float32)).astype(jnp.bfloat16)

    return call(
        kernel,
        [VMEM, VMEM, VMEM, VMEM],
        jax.ShapeDtypeStruct((3, seq * per, count), jnp.bfloat16),
        1 << 24,
        name="last_grads",
    )(grad_mixed, middle, grad_gated, projected)


def turn(array, by):
    by = by % array.shape[0]
    return array if by == 0 else jnp.concatenate([array[by:], array[:by]], axis=0)


def causal(given, skip):
    chunks, rows, _ = given.shape
    per = rows // 3

    def kernel(skip_ref, given_ref, inner_ref, toeplitz_ref, wide, shifted, collected):
        wide[...] = given_ref[...].astype(jnp.float32).reshape(chunks * rows, BLOCK)
        for part in range(2):
            shifted[part, pl.ds(0, chunks), :] = jnp.zeros((chunks, BLOCK), jnp.float32)
        upper = lax.broadcasted_iota(jnp.int32, (BLOCK, BLOCK), 1) >= lax.broadcasted_iota(
            jnp.int32, (BLOCK, BLOCK), 0
        )

        @pl.loop(0, per)
        def _(channel):
            def take(which):
                return turn(wide[pl.ds(which * per + channel, chunks, stride=rows), :], -FIRST_SEQ)

            mixed, taps = take(0) * take(1), take(2)
            near = mixed.astype(jnp.bfloat16).astype(jnp.float32)
            shifted[0, pl.ds(chunks, chunks), :] = near
            shifted[1, pl.ds(chunks, chunks), :] = mixed - near
            before = jnp.zeros((BLOCK, BLOCK), jnp.float32)
            total = jnp.zeros((2 * chunks, BLOCK), jnp.float32)
            for lag in range(0, chunks, 2):
                blocks, signals = [], []
                for one in (lag, lag + 1):
                    spread = jnp.broadcast_to(taps[one : one + 1, :], (BLOCK, BLOCK))
                    turned = pltpu.roll(spread, 0, 1, stride=1, stride_axis=0)
                    block = jnp.where(upper, turned, before).astype(jnp.bfloat16)
                    before = turned
                    toeplitz_ref[channel, :, one * BLOCK : (one + 1) * BLOCK] = block
                    blocks.append(block)
                    parts = [shifted[part, chunks - one : 2 * chunks - one, :] for part in range(2)]
                    signals.append(jnp.concatenate(parts, axis=0).astype(jnp.bfloat16))
                total = total + jnp.dot(
                    jnp.concatenate(signals, axis=1),
                    jnp.concatenate(blocks, axis=0),
                    preferred_element_type=jnp.float32,
                )
            inner = total[:chunks] + total[chunks:] + skip_ref[channel] * mixed
            collected[pl.ds(channel, chunks, stride=per), :] = turn(inner, FIRST_SEQ)

        inner_ref[...] = collected[...].astype(jnp.bfloat16).reshape(inner_ref.shape)

    return call(
        kernel,
        [SMEM, VMEM],
        [
            jax.ShapeDtypeStruct((chunks // 2, 2 * per, BLOCK), jnp.bfloat16),
            jax.ShapeDtypeStruct((per, BLOCK, chunks * BLOCK), jnp.bfloat16),
        ],
        16 * per * chunks * chunks * BLOCK * BLOCK,
        [
            pltpu.VMEM((chunks * rows, BLOCK), jnp.float32),
            pltpu.VMEM((2, 2 * chunks, BLOCK), jnp.float32),
            pltpu.VMEM((chunks * per, BLOCK), jnp.float32),
        ],
        "causal_sum",
    )(skip, given)


def adjoint(back, toeplitz, skip):
    chunks, rows, _ = back.shape
    per = rows // 2

    def kernel(skip_ref, back_ref, toeplitz_ref, out_ref, grads, shifted, collected):
        grads[...] = back_ref[...].astype(jnp.float32).reshape(chunks * rows, BLOCK)
        shifted[pl.ds(chunks, chunks), :] = jnp.zeros((chunks, BLOCK), jnp.float32)

        @pl.loop(0, per)
        def _(channel):
            grad_inner = turn(grads[pl.ds(per + channel, chunks, stride=rows), :], -FIRST_SEQ)
            shifted[pl.ds(0, chunks), :] = grad_inner
            total = jnp.zeros((chunks, BLOCK), jnp.float32)
            for lag in range(0, chunks, 2):
                signals = [shifted[one : one + chunks, :] for one in (lag, lag + 1)]
                total = total + lax.dot_general(
                    jnp.concatenate(signals, axis=1).astype(jnp.bfloat16),
                    toeplitz_ref[channel, :, lag * BLOCK : (lag + 2) * BLOCK],
                    LANES,
                    preferred_element_type=jnp.float32,
                )
            grad_mixed = total + skip_ref[channel] * grad_inner
            collected[pl.ds(channel, chunks, stride=per), :] = turn(grad_mixed, FIRST_SEQ)

        out_ref[...] = collected[...].astype(jnp.bfloat16).reshape(out_ref.shape)

    return call(
        kernel,
        [SMEM, VMEM, VMEM],
        jax.ShapeDtypeStruct((chunks // 2, 2 * per, BLOCK), jnp.bfloat16),
        16 * per * chunks * chunks * BLOCK * BLOCK,
        [
            pltpu.VMEM((chunks * rows, BLOCK), jnp.float32),
            pltpu.VMEM((2 * chunks, BLOCK), jnp.float32),
            pltpu.VMEM((chunks * per, BLOCK), jnp.float32),
        ],
        "adjoint_sum",
    )(skip, back, toeplitz)


def per_device(projected, filters, skip, out_weight, cotangent):
    seq = lax.axis_size("seq")
    chan = lax.axis_size("chan")
    planes = chan // 2
    channels, count = filters.shape
    per = channels // seq
    half = lax.axis_index("chan") & 1
    own, other = half.reshape(1), (1 - half).reshape(1)
    along_z = [[2 * z + h for z in range(planes)] for h in range(2)]
    pairs = [(i, i ^ 1) for i in range(chan)]

    def exchange_seq(array):
        groups = [[(place + FIRST_SEQ) % seq for place in range(seq)]]
        return lax.all_to_all(array, "seq", 0, 0, tiled=True, axis_index_groups=groups)

    def exchange_z(array, first=0):
        groups = [group[first:] + group[:first] for group in along_z]
        return lax.all_to_all(array, "chan", 0, 0, tiled=True, axis_index_groups=groups)

    weight = out_weight.reshape(planes, 2, channels, out_weight.shape[1])
    share_other, packed = first(other, weight, cotangent, projected, filters, seq)
    received = lax.ppermute(share_other, "chan", pairs)
    given = exchange_seq(packed)
    share_own = partial_half(own, weight, cotangent, jnp.float32)
    skip_here = lax.dynamic_slice(skip, ((lax.axis_index("seq") - FIRST_SEQ) % seq * per,), (per,))
    inner, toeplitz = causal(given, skip_here)
    shares = exchange_z(total_share(share_own, received, FIRST_SUM), FIRST_SUM)
    packed, grad_gated = pack_middle(inner, shares, projected, seq)
    middle = exchange_seq(packed)
    gated_half = exchange_z(spread(middle, projected, planes), FIRST_GATED)
    grads_there = adjoint(middle, toeplitz, skip_here)
    grads_there, gated_half = lax.optimization_barrier((grads_there, gated_half))
    gated_other = lax.ppermute(gated_half, "chan", pairs)
    output, weight_other = project_half(own, gated_half, weight, FIRST_GATED)
    grads = exchange_seq(grads_there.reshape(seq, per, count))
    output = project_half(other, gated_other, weight_other, FIRST_GATED, output)
    grads, output = lax.optimization_barrier((grads, output))
    grads = last_grads(grads.reshape(seq // 2, 2 * per, count), middle, grad_gated, projected)
    return output, grads


def solution(mesh):
    in_specs = (
        P(None, "chan", "seq"),
        P("chan", "seq"),
        P("chan"),
        P(None, "chan"),
        P("seq", "chan"),
    )
    out_specs = (P("seq", "chan"), P(None, "chan", "seq"))
    return jax.shard_map(
        per_device, mesh=mesh, in_specs=in_specs, out_specs=out_specs, check_vma=False
    )
```

```python
import jax
import jax.numpy as jnp
from jax import lax
from jax.experimental import pallas as pl
from jax.experimental.pallas import tpu as pltpu
from jax.sharding import PartitionSpec as P

BLOCK = 128
LANES = (((1,), (1,)), ((), ()))
ROWS = (((0,), (0,)), ((), ()))
VMEM_LIMIT = 8 << 20
FIRST_LIMIT = 54 << 20
FIRST_SUM = 6
FIRST_GATED = 5
FIRST_SEQ = 19
VMEM = pl.BlockSpec(memory_space=pltpu.VMEM)
HBM = pl.BlockSpec(memory_space=pltpu.HBM)
SMEM = pl.BlockSpec(memory_space=pltpu.SMEM)


def call(kernel, in_specs, out_shape, flops, scratch=(), name=None, limit=VMEM_LIMIT, out=VMEM):
    return pl.pallas_call(
        kernel,
        in_specs=in_specs,
        out_specs=jax.tree.map(lambda _: out, out_shape),
        out_shape=out_shape,
        scratch_shapes=list(scratch),
        compiler_params=pltpu.CompilerParams(vmem_limit_bytes=limit),
        cost_estimate=pl.CostEstimate(flops=flops, bytes_accessed=4 << 20, transcendentals=0),
        name=name,
    )


def partial_half(half, weight, cotangent, dtype):
    planes, _, rows, width = weight.shape
    count = cotangent.shape[0]

    def kernel(half_ref, weight_ref, cotangent_ref, out_ref):
        for plane in range(planes):
            out_ref[plane] = lax.dot_general(
                weight_ref[plane, half_ref[0]],
                cotangent_ref[...],
                LANES,
                preferred_element_type=jnp.float32,
            ).astype(dtype)

    return call(
        kernel,
        [SMEM, VMEM, VMEM],
        jax.ShapeDtypeStruct((planes, rows, count), dtype),
        2 * planes * rows * width * count,
        name="partial_grad_gated",
    )(half, weight, cotangent)


def total_share(share, received, first):
    planes = share.shape[0]

    def kernel(share_ref, received_ref, out_ref):
        for place in range(planes):
            plane = (place + first) % planes
            total = share_ref[plane] + received_ref[plane].astype(jnp.float32)
            out_ref[place] = total.astype(jnp.bfloat16)

    return call(
        kernel,
        [VMEM, VMEM],
        jax.ShapeDtypeStruct(share.shape, jnp.bfloat16),
        1 << 24,
        name="total_share",
    )(share, received)


def project_half(half, gated, weight, first, before=None):
    planes, rows, width = weight.shape[0], weight.shape[-2], weight.shape[-1]
    count = gated.shape[-1]
    result = jax.ShapeDtypeStruct((count, width), jnp.float32 if before is None else jnp.bfloat16)

    def early(half_ref, gated_ref, weight_ref, out_ref, kept_ref, moved):
        copies = [
            pltpu.make_async_copy(
                weight_ref.at[(plane + first) % planes, 1 - half_ref[0]],
                kept_ref.at[plane],
                moved.at[plane],
            )
            for plane in range(planes)
        ]
        for copy in copies:
            copy.start()
        total = jnp.zeros((count, width), jnp.float32)
        for plane in range(planes):
            total = total + lax.dot_general(
                gated_ref[plane],
                weight_ref[(plane + first) % planes, half_ref[0]],
                ROWS,
                preferred_element_type=jnp.float32,
            )
        out_ref[...] = total
        for copy in copies:
            copy.wait()

    def late(gated_ref, weight_ref, before_ref, out_ref):
        total = before_ref[...] + lax.dot_general(
            gated_ref[...].reshape(planes * rows, count),
            weight_ref[...].reshape(planes * rows, width),
            ROWS,
            preferred_element_type=jnp.float32,
        )
        out_ref[...] = total.astype(out_ref.dtype)

    flops = 2 * planes * rows * width * count
    if before is None:
        kept = jax.ShapeDtypeStruct((planes, rows, width), weight.dtype)
        return call(
            early,
            [SMEM, VMEM, VMEM],
            [result, kept],
            flops,
            [pltpu.SemaphoreType.DMA((planes,))],
            name="output_early",
        )(half, gated, weight)
    return call(late, [VMEM] * 3, result, flops, name="output_late")(gated, weight, before)


def first(half, weight, cotangent, projected, filters, seq):
    planes, _, rows, width = weight.shape
    _, channels, count = projected.shape
    per = channels // seq

    def kernel(
        half_ref,
        weight_ref,
        cotangent_ref,
        projected_ref,
        filters_ref,
        share_ref,
        packed_ref,
        weight_here,
        cotangent_here,
        projected_here,
        filters_here,
        share_here,
        packed_here,
        arrived,
        left,
    ):
        places = [
            (projected_ref.at[pl.ds(1, 2)], projected_here),
            (filters_ref, filters_here),
            (cotangent_ref, cotangent_here),
        ]
        group = planes // 2
        places += [
            (weight_ref.at[pl.ds(start, group), half_ref[0]], weight_here.at[pl.ds(start, group)])
            for start in (0, group)
        ]
        copies = [
            pltpu.make_async_copy(source, target, arrived.at[i])
            for i, (source, target) in enumerate(places)
        ]
        for copy in copies:
            copy.start()
        copies[0].wait()
        copies[1].wait()
        parts = [projected_here[which].astype(jnp.float32) for which in range(2)]
        parts = [part.reshape(seq, per, count) for part in parts + [filters_here[...]]]
        packed_here[...] = jnp.concatenate(parts, axis=1).astype(jnp.bfloat16)
        leaving = [pltpu.make_async_copy(packed_here, packed_ref, left.at[2])]
        leaving[0].start()
        copies[2].wait()
        for place, start in enumerate((0, group)):
            copies[3 + place].wait()
            share = lax.dot_general(
                weight_here[pl.ds(start, group)].reshape(group * rows, width),
                cotangent_here[...],
                LANES,
                preferred_element_type=jnp.float32,
            )
            share_here[pl.ds(start, group)] = share.astype(jnp.bfloat16).reshape(group, rows, count)
            leaving.append(
                pltpu.make_async_copy(
                    share_here.at[pl.ds(start, group)],
                    share_ref.at[pl.ds(start, group)],
                    left.at[place],
                )
            )
            leaving[-1].start()
        for copy in leaving:
            copy.wait()

    return call(
        kernel,
        [SMEM, HBM, HBM, HBM, HBM],
        [
            jax.ShapeDtypeStruct((planes, rows, count), jnp.bfloat16),
            jax.ShapeDtypeStruct((seq, 3 * per, count), jnp.bfloat16),
        ],
        2 * planes * rows * width * count,
        [
            pltpu.VMEM((planes, rows, width), weight.dtype),
            pltpu.VMEM(cotangent.shape, cotangent.dtype),
            pltpu.VMEM((2, channels, count), projected.dtype),
            pltpu.VMEM(filters.shape, filters.dtype),
            pltpu.VMEM((planes, rows, count), jnp.bfloat16),
            pltpu.VMEM((seq, 3 * per, count), jnp.bfloat16),
            pltpu.SemaphoreType.DMA((5,)),
            pltpu.SemaphoreType.DMA((3,)),
        ],
        "first_share",
        FIRST_LIMIT,
        HBM,
    )(half, weight, cotangent, projected, filters)


def pack_middle(inner, shares, projected, seq):
    planes, channels, count = shares.shape
    per = channels // seq

    def kernel(inner_ref, shares_ref, projected_ref, out_ref, total_ref):
        total = shares_ref[0].astype(jnp.float32)
        for plane in range(1, planes):
            total = total + shares_ref[plane].astype(jnp.float32)
        total_ref[...] = total
        back = (total * projected_ref[0].astype(jnp.float32)).reshape(seq, per, count)
        there = inner_ref[...].astype(jnp.float32).reshape(seq, per, count)
        out_ref[...] = jnp.concatenate([there, back], axis=1).astype(jnp.bfloat16)

    return call(
        kernel,
        [VMEM, VMEM, VMEM],
        [
            jax.ShapeDtypeStruct((seq, 2 * per, count), jnp.bfloat16),
            jax.ShapeDtypeStruct((channels, count), jnp.float32),
        ],
        1 << 24,
        name="pack_middle",
    )(inner, shares, projected)


def spread(middle, projected, planes):
    seq, rows, count = middle.shape
    per = rows // 2

    def kernel(middle_ref, projected_ref, out_ref, gated, left):
        inner = middle_ref[...].astype(jnp.float32)[:, :per].reshape(seq * per, count)
        gated[...] = (projected_ref[0].astype(jnp.float32) * inner).astype(jnp.bfloat16)
        copies = [
            pltpu.make_async_copy(gated, out_ref.at[plane], left.at[plane])
            for plane in range(planes)
        ]
        for copy in copies:
            copy.start()
        for copy in copies:
            copy.wait()

    return call(
        kernel,
        [VMEM, VMEM],
        jax.ShapeDtypeStruct((planes, seq * per, count), jnp.bfloat16),
        1 << 24,
        [pltpu.VMEM((seq * per, count), jnp.bfloat16), pltpu.SemaphoreType.DMA((planes,))],
        "spread_gated",
        out=HBM,
    )(middle, projected)


def last_grads(grad_mixed, middle, grad_gated, projected):
    seq, rows, count = middle.shape
    per = rows // 2

    def kernel(grad_mixed_ref, middle_ref, grad_gated_ref, projected_ref, out_ref):
        inner = middle_ref[...].astype(jnp.float32)[:, :per].reshape(seq * per, count)
        mixed = grad_mixed_ref[...].astype(jnp.float32).reshape(seq * per, count)
        out_ref[0] = (grad_gated_ref[...] * inner).astype(jnp.bfloat16)
        out_ref[1] = (mixed * projected_ref[2].astype(jnp.float32)).astype(jnp.bfloat16)
        out_ref[2] = (mixed * projected_ref[1].astype(jnp.float32)).astype(jnp.bfloat16)

    return call(
        kernel,
        [VMEM, VMEM, VMEM, VMEM],
        jax.ShapeDtypeStruct((3, seq * per, count), jnp.bfloat16),
        1 << 24,
        name="last_grads",
    )(grad_mixed, middle, grad_gated, projected)


def turn(array, by):
    by = by % array.shape[0]
    return array if by == 0 else jnp.concatenate([array[by:], array[:by]], axis=0)


def toeplitz_block(taps, lag, before, upper):
    spread = jnp.broadcast_to(taps[lag : lag + 1, :], (BLOCK, BLOCK))
    turned = pltpu.roll(spread, 0, 1, stride=1, stride_axis=0)
    return jnp.where(upper, turned, before).astype(jnp.bfloat16), turned


def upper_half():
    sub, lane = (lax.broadcasted_iota(jnp.int32, (BLOCK, BLOCK), axis) for axis in range(2))
    return lane >= sub


def causal(given, skip):
    chunks, rows, _ = given.shape
    per = rows // 3

    def kernel(skip_ref, given_ref, inner_ref, wide, shifted, collected):
        wide[pl.ds(0, chunks * rows), :] = (
            given_ref[...].astype(jnp.float32).reshape(chunks * rows, BLOCK)
        )
        for part in range(2):
            shifted[part, pl.ds(0, chunks), :] = jnp.zeros((chunks, BLOCK), jnp.float32)
        upper = upper_half()

        @pl.loop(0, per)
        def _(channel):
            def take(which):
                return turn(wide[pl.ds(which * per + channel, chunks, stride=rows), :], -FIRST_SEQ)

            mixed, taps = take(0) * take(1), take(2)
            near = mixed.astype(jnp.bfloat16).astype(jnp.float32)
            shifted[0, pl.ds(chunks, chunks), :] = near
            shifted[1, pl.ds(chunks, chunks), :] = mixed - near
            before = jnp.zeros((BLOCK, BLOCK), jnp.float32)
            total = jnp.zeros((2 * chunks, BLOCK), jnp.float32)
            for lag in range(0, chunks, 2):
                blocks, signals = [], []
                for one in (lag, lag + 1):
                    block, before = toeplitz_block(taps, one, before, upper)
                    blocks.append(block)
                    parts = [shifted[part, chunks - one : 2 * chunks - one, :] for part in range(2)]
                    signals.append(jnp.concatenate(parts, axis=0).astype(jnp.bfloat16))
                total = total + jnp.dot(
                    jnp.concatenate(signals, axis=1),
                    jnp.concatenate(blocks, axis=0),
                    preferred_element_type=jnp.float32,
                )
            inner = total[:chunks] + total[chunks:] + skip_ref[channel] * mixed
            collected[pl.ds(channel, chunks, stride=per), :] = turn(inner, FIRST_SEQ)

        inner = collected[pl.ds(0, chunks * per), :]
        inner_ref[...] = inner.astype(jnp.bfloat16).reshape(inner_ref.shape)

    return call(
        kernel,
        [SMEM, VMEM],
        jax.ShapeDtypeStruct((chunks // 2, 2 * per, BLOCK), jnp.bfloat16),
        16 * per * chunks * chunks * BLOCK * BLOCK,
        [
            pltpu.VMEM(((chunks + 1) * rows, BLOCK), jnp.float32),
            pltpu.VMEM((2, 2 * chunks, BLOCK), jnp.float32),
            pltpu.VMEM(((chunks + 1) * per, BLOCK), jnp.float32),
        ],
        "causal_sum",
    )(skip, given)


def adjoint(given, back, skip):
    chunks, rows, _ = back.shape
    per = rows // 2
    wide_rows = given.shape[1]

    def kernel(skip_ref, given_ref, back_ref, out_ref, wide, grads, shifted, collected):
        wide[pl.ds(0, chunks * wide_rows), :] = (
            given_ref[...].astype(jnp.float32).reshape(chunks * wide_rows, BLOCK)
        )
        upper = upper_half()
        grads[pl.ds(0, chunks * rows), :] = (
            back_ref[...].astype(jnp.float32).reshape(chunks * rows, BLOCK)
        )
        shifted[pl.ds(chunks, chunks), :] = jnp.zeros((chunks, BLOCK), jnp.float32)

        @pl.loop(0, per)
        def _(channel):
            grad_inner = turn(grads[pl.ds(per + channel, chunks, stride=rows), :], -FIRST_SEQ)
            shifted[pl.ds(0, chunks), :] = grad_inner
            taps = turn(wide[pl.ds(2 * per + channel, chunks, stride=wide_rows), :], -FIRST_SEQ)
            before = jnp.zeros((BLOCK, BLOCK), jnp.float32)
            total = jnp.zeros((chunks, BLOCK), jnp.float32)
            for lag in range(0, chunks, 2):
                blocks, signals = [], []
                for one in (lag, lag + 1):
                    block, before = toeplitz_block(taps, one, before, upper)
                    blocks.append(block)
                    signals.append(shifted[one : one + chunks, :])
                total = total + lax.dot_general(
                    jnp.concatenate(signals, axis=1).astype(jnp.bfloat16),
                    jnp.concatenate(blocks, axis=1),
                    LANES,
                    preferred_element_type=jnp.float32,
                )
            grad_mixed = total + skip_ref[channel] * grad_inner
            collected[pl.ds(channel, chunks, stride=per), :] = turn(grad_mixed, FIRST_SEQ)

        mixed = collected[pl.ds(0, chunks * per), :]
        out_ref[...] = mixed.astype(jnp.bfloat16).reshape(out_ref.shape)

    return call(
        kernel,
        [SMEM, VMEM, VMEM],
        jax.ShapeDtypeStruct((chunks // 2, 2 * per, BLOCK), jnp.bfloat16),
        16 * per * chunks * chunks * BLOCK * BLOCK,
        [
            pltpu.VMEM(((chunks + 1) * wide_rows, BLOCK), jnp.float32),
            pltpu.VMEM(((chunks + 1) * rows, BLOCK), jnp.float32),
            pltpu.VMEM((2 * chunks, BLOCK), jnp.float32),
            pltpu.VMEM(((chunks + 1) * per, BLOCK), jnp.float32),
        ],
        "adjoint_sum",
    )(skip, given, back)


def per_device(projected, filters, skip, out_weight, cotangent):
    seq = lax.axis_size("seq")
    chan = lax.axis_size("chan")
    planes = chan // 2
    channels, count = filters.shape
    per = channels // seq
    half = lax.axis_index("chan") & 1
    own, other = half.reshape(1), (1 - half).reshape(1)
    along_z = [[2 * z + h for z in range(planes)] for h in range(2)]
    pairs = [(i, i ^ 1) for i in range(chan)]

    def exchange_seq(array):
        groups = [[(place + FIRST_SEQ) % seq for place in range(seq)]]
        return lax.all_to_all(array, "seq", 0, 0, tiled=True, axis_index_groups=groups)

    def exchange_z(array, first=0):
        groups = [group[first:] + group[:first] for group in along_z]
        return lax.all_to_all(array, "chan", 0, 0, tiled=True, axis_index_groups=groups)

    weight = out_weight.reshape(planes, 2, channels, out_weight.shape[1])
    share_other, packed = first(other, weight, cotangent, projected, filters, seq)
    received = lax.ppermute(share_other, "chan", pairs)
    given = exchange_seq(packed)
    share_own = partial_half(own, weight, cotangent, jnp.float32)
    skip_here = lax.dynamic_slice(skip, ((lax.axis_index("seq") - FIRST_SEQ) % seq * per,), (per,))
    inner = causal(given, skip_here)
    shares = exchange_z(total_share(share_own, received, FIRST_SUM), FIRST_SUM)
    packed, grad_gated = pack_middle(inner, shares, projected, seq)
    middle = exchange_seq(packed)
    gated_half = exchange_z(spread(middle, projected, planes), FIRST_GATED)
    grads_there = adjoint(given, middle, skip_here)
    grads_there, gated_half = lax.optimization_barrier((grads_there, gated_half))
    gated_other = lax.ppermute(gated_half, "chan", pairs)
    output, weight_other = project_half(own, gated_half, weight, FIRST_GATED)
    grads = exchange_seq(grads_there.reshape(seq, per, count))
    output = project_half(other, gated_other, weight_other, FIRST_GATED, output)
    grads, output = lax.optimization_barrier((grads, output))
    grads = last_grads(grads.reshape(seq // 2, 2 * per, count), middle, grad_gated, projected)
    return output, grads


def solution(mesh):
    in_specs = (
        P(None, "chan", "seq"),
        P("chan", "seq"),
        P("chan"),
        P(None, "chan"),
        P("seq", "chan"),
    )
    out_specs = (P("seq", "chan"), P(None, "chan", "seq"))
    return jax.shard_map(
        per_device, mesh=mesh, in_specs=in_specs, out_specs=out_specs, check_vma=False
    )
```

```python
import jax
import jax.numpy as jnp
from jax import lax
from jax.experimental import pallas as pl
from jax.experimental.pallas import tpu as pltpu
from jax.sharding import PartitionSpec as P

BLOCK = 128
LANES = (((1,), (1,)), ((), ()))
ROWS = (((0,), (0,)), ((), ()))
VMEM_LIMIT = 8 << 20
FIRST_LIMIT = 54 << 20
FIRST_SUM = 6
FIRST_GATED = 5
FIRST_SEQ = 19
VMEM = pl.BlockSpec(memory_space=pltpu.VMEM)
HBM = pl.BlockSpec(memory_space=pltpu.HBM)
SMEM = pl.BlockSpec(memory_space=pltpu.SMEM)


def call(kernel, in_specs, out_shape, flops, scratch=(), name=None, limit=VMEM_LIMIT, out=VMEM):
    return pl.pallas_call(
        kernel,
        in_specs=in_specs,
        out_specs=jax.tree.map(lambda _: out, out_shape),
        out_shape=out_shape,
        scratch_shapes=list(scratch),
        compiler_params=pltpu.CompilerParams(vmem_limit_bytes=limit),
        cost_estimate=pl.CostEstimate(flops=flops, bytes_accessed=4 << 20, transcendentals=0),
        name=name,
    )


def partial_half(half, weight, cotangent, dtype):
    planes, _, rows, width = weight.shape
    count = cotangent.shape[0]

    def kernel(half_ref, weight_ref, cotangent_ref, out_ref):
        for plane in range(planes):
            out_ref[plane] = lax.dot_general(
                weight_ref[plane, half_ref[0]],
                cotangent_ref[...],
                LANES,
                preferred_element_type=jnp.float32,
            ).astype(dtype)

    return call(
        kernel,
        [SMEM, VMEM, VMEM],
        jax.ShapeDtypeStruct((planes, rows, count), dtype),
        2 * planes * rows * width * count,
        name="partial_grad_gated",
    )(half, weight, cotangent)


def total_share(share, received, first):
    planes = share.shape[0]

    def kernel(share_ref, received_ref, out_ref):
        for place in range(planes):
            plane = (place + first) % planes
            total = share_ref[plane] + received_ref[plane].astype(jnp.float32)
            out_ref[place] = total.astype(jnp.bfloat16)

    return call(
        kernel,
        [VMEM, VMEM],
        jax.ShapeDtypeStruct(share.shape, jnp.bfloat16),
        1 << 24,
        name="total_share",
    )(share, received)


def project_half(half, gated, weight, first, before=None):
    planes, rows, width = weight.shape[0], weight.shape[-2], weight.shape[-1]
    count = gated.shape[-1]
    result = jax.ShapeDtypeStruct((count, width), jnp.float32 if before is None else jnp.bfloat16)

    def early(half_ref, gated_ref, weight_ref, out_ref, kept_ref, moved):
        copies = [
            pltpu.make_async_copy(
                weight_ref.at[lax.rem(half_ref[1] + 1 + plane, planes), 1 - half_ref[0]],
                kept_ref.at[plane],
                moved.at[plane],
            )
            for plane in range(planes)
        ]
        for copy in copies:
            copy.start()
        total = jnp.zeros((count, width), jnp.float32)
        for plane in range(planes):
            total = total + lax.dot_general(
                gated_ref[plane],
                weight_ref[(plane + first) % planes, half_ref[0]],
                ROWS,
                preferred_element_type=jnp.float32,
            )
        out_ref[...] = total
        for copy in copies:
            copy.wait()

    def late(gated_ref, near_ref, weight_ref, before_ref, out_ref):
        others = planes - 1
        total = before_ref[...] + lax.dot_general(
            near_ref[...], weight_ref[others], ROWS, preferred_element_type=jnp.float32
        )
        total = total + lax.dot_general(
            gated_ref[...].reshape(others * rows, count),
            weight_ref[pl.ds(0, others)].reshape(others * rows, width),
            ROWS,
            preferred_element_type=jnp.float32,
        )
        out_ref[...] = total.astype(out_ref.dtype)

    flops = 2 * planes * rows * width * count
    if before is None:
        kept = jax.ShapeDtypeStruct((planes, rows, width), weight.dtype)
        return call(
            early,
            [SMEM, VMEM, VMEM],
            [result, kept],
            flops,
            [pltpu.SemaphoreType.DMA((planes,))],
            name="output_early",
        )(half, gated, weight)
    return call(late, [VMEM] * 4, result, flops, name="output_late")(gated, *half, weight, before)


def first(half, weight, cotangent, projected, filters, seq):
    planes, _, rows, width = weight.shape
    _, channels, count = projected.shape
    per = channels // seq

    def kernel(
        half_ref,
        weight_ref,
        cotangent_ref,
        projected_ref,
        filters_ref,
        share_ref,
        packed_ref,
        weight_here,
        cotangent_here,
        projected_here,
        filters_here,
        share_here,
        packed_here,
        arrived,
        left,
    ):
        places = [
            (projected_ref.at[pl.ds(1, 2)], projected_here),
            (filters_ref, filters_here),
            (cotangent_ref, cotangent_here),
        ]
        group = planes // 2
        places += [
            (weight_ref.at[pl.ds(start, group), half_ref[0]], weight_here.at[pl.ds(start, group)])
            for start in (0, group)
        ]
        copies = [
            pltpu.make_async_copy(source, target, arrived.at[i])
            for i, (source, target) in enumerate(places)
        ]
        for copy in copies:
            copy.start()
        copies[0].wait()
        copies[1].wait()
        parts = [projected_here[which].astype(jnp.float32) for which in range(2)]
        parts = [part.reshape(seq, per, count) for part in parts + [filters_here[...]]]
        packed_here[...] = jnp.concatenate(parts, axis=1).astype(jnp.bfloat16)
        leaving = [pltpu.make_async_copy(packed_here, packed_ref, left.at[2])]
        leaving[0].start()
        copies[2].wait()
        for place, start in enumerate((0, group)):
            copies[3 + place].wait()
            share = lax.dot_general(
                weight_here[pl.ds(start, group)].reshape(group * rows, width),
                cotangent_here[...],
                LANES,
                preferred_element_type=jnp.float32,
            )
            share_here[pl.ds(start, group)] = share.astype(jnp.bfloat16).reshape(group, rows, count)
            leaving.append(
                pltpu.make_async_copy(
                    share_here.at[pl.ds(start, group)],
                    share_ref.at[pl.ds(start, group)],
                    left.at[place],
                )
            )
            leaving[-1].start()
        for copy in leaving:
            copy.wait()

    return call(
        kernel,
        [SMEM, HBM, HBM, HBM, HBM],
        [
            jax.ShapeDtypeStruct((planes, rows, count), jnp.bfloat16),
            jax.ShapeDtypeStruct((seq, 3 * per, count), jnp.bfloat16),
        ],
        2 * planes * rows * width * count,
        [
            pltpu.VMEM((planes, rows, width), weight.dtype),
            pltpu.VMEM(cotangent.shape, cotangent.dtype),
            pltpu.VMEM((2, channels, count), projected.dtype),
            pltpu.VMEM(filters.shape, filters.dtype),
            pltpu.VMEM((planes, rows, count), jnp.bfloat16),
            pltpu.VMEM((seq, 3 * per, count), jnp.bfloat16),
            pltpu.SemaphoreType.DMA((5,)),
            pltpu.SemaphoreType.DMA((3,)),
        ],
        "first_share",
        FIRST_LIMIT,
        HBM,
    )(half, weight, cotangent, projected, filters)


def pack_middle(inner, shares, projected, seq):
    planes, channels, count = shares.shape
    per = channels // seq

    def kernel(inner_ref, shares_ref, projected_ref, out_ref, total_ref):
        total = shares_ref[0].astype(jnp.float32)
        for plane in range(1, planes):
            total = total + shares_ref[plane].astype(jnp.float32)
        total_ref[...] = total
        back = (total * projected_ref[0].astype(jnp.float32)).reshape(seq, per, count)
        there = inner_ref[...].astype(jnp.float32).reshape(seq, per, count)
        out_ref[...] = jnp.concatenate([there, back], axis=1).astype(jnp.bfloat16)

    return call(
        kernel,
        [VMEM, VMEM, VMEM],
        [
            jax.ShapeDtypeStruct((seq, 2 * per, count), jnp.bfloat16),
            jax.ShapeDtypeStruct((channels, count), jnp.float32),
        ],
        1 << 24,
        name="pack_middle",
    )(inner, shares, projected)


def spread(middle, projected, planes):
    seq, rows, count = middle.shape
    per = rows // 2

    def kernel(middle_ref, projected_ref, out_ref, gated, left):
        inner = middle_ref[...].astype(jnp.float32)[:, :per].reshape(seq * per, count)
        gated[...] = (projected_ref[0].astype(jnp.float32) * inner).astype(jnp.bfloat16)
        copies = [
            pltpu.make_async_copy(gated, out_ref.at[plane], left.at[plane])
            for plane in range(planes)
        ]
        for copy in copies:
            copy.start()
        for copy in copies:
            copy.wait()

    return call(
        kernel,
        [VMEM, VMEM],
        jax.ShapeDtypeStruct((planes, seq * per, count), jnp.bfloat16),
        1 << 24,
        [pltpu.VMEM((seq * per, count), jnp.bfloat16), pltpu.SemaphoreType.DMA((planes,))],
        "spread_gated",
        out=HBM,
    )(middle, projected)


def other_planes(start, gated):
    planes, channels, count = gated.shape

    def kernel(start_ref, gated_ref, out_ref, moved):
        copies = [
            pltpu.make_async_copy(
                gated_ref.at[lax.rem(start_ref[0] + place, planes)],
                out_ref.at[place],
                moved.at[place],
            )
            for place in range(planes - 1)
        ]
        for copy in copies:
            copy.start()
        for copy in copies:
            copy.wait()

    return call(
        kernel,
        [SMEM, VMEM],
        jax.ShapeDtypeStruct((planes - 1, channels, count), gated.dtype),
        1 << 22,
        [pltpu.SemaphoreType.DMA((planes - 1,))],
        "other_planes",
    )(start, gated)


def last_grads(grad_mixed, middle, grad_gated, projected):
    seq, rows, count = middle.shape
    per = rows // 2

    def kernel(grad_mixed_ref, middle_ref, grad_gated_ref, projected_ref, out_ref):
        inner = middle_ref[...].astype(jnp.float32)[:, :per].reshape(seq * per, count)
        mixed = grad_mixed_ref[...].astype(jnp.float32).reshape(seq * per, count)
        out_ref[0] = (grad_gated_ref[...] * inner).astype(jnp.bfloat16)
        out_ref[1] = (mixed * projected_ref[2].astype(jnp.float32)).astype(jnp.bfloat16)
        out_ref[2] = (mixed * projected_ref[1].astype(jnp.float32)).astype(jnp.bfloat16)

    return call(
        kernel,
        [VMEM, VMEM, VMEM, VMEM],
        jax.ShapeDtypeStruct((3, seq * per, count), jnp.bfloat16),
        1 << 24,
        name="last_grads",
    )(grad_mixed, middle, grad_gated, projected)


def turn(array, by):
    by = by % array.shape[0]
    return array if by == 0 else jnp.concatenate([array[by:], array[:by]], axis=0)


def toeplitz_block(taps, lag, before, upper):
    spread = jnp.broadcast_to(taps[lag : lag + 1, :], (BLOCK, BLOCK))
    turned = pltpu.roll(spread, 0, 1, stride=1, stride_axis=0)
    return jnp.where(upper, turned, before).astype(jnp.bfloat16), turned


def upper_half():
    sub, lane = (lax.broadcasted_iota(jnp.int32, (BLOCK, BLOCK), axis) for axis in range(2))
    return lane >= sub


def causal(given, skip):
    chunks, rows, _ = given.shape
    per = rows // 3

    def kernel(skip_ref, given_ref, inner_ref, wide, shifted, collected):
        wide[pl.ds(0, chunks * rows), :] = (
            given_ref[...].astype(jnp.float32).reshape(chunks * rows, BLOCK)
        )
        for part in range(2):
            shifted[part, pl.ds(0, chunks), :] = jnp.zeros((chunks, BLOCK), jnp.float32)
        upper = upper_half()

        @pl.loop(0, per)
        def _(channel):
            def take(which):
                return turn(wide[pl.ds(which * per + channel, chunks, stride=rows), :], -FIRST_SEQ)

            mixed, taps = take(0) * take(1), take(2)
            near = mixed.astype(jnp.bfloat16).astype(jnp.float32)
            shifted[0, pl.ds(chunks, chunks), :] = near
            shifted[1, pl.ds(chunks, chunks), :] = mixed - near
            before = jnp.zeros((BLOCK, BLOCK), jnp.float32)
            total = jnp.zeros((2 * chunks, BLOCK), jnp.float32)
            for lag in range(0, chunks, 2):
                blocks, signals = [], []
                for one in (lag, lag + 1):
                    block, before = toeplitz_block(taps, one, before, upper)
                    blocks.append(block)
                    parts = [shifted[part, chunks - one : 2 * chunks - one, :] for part in range(2)]
                    signals.append(jnp.concatenate(parts, axis=0).astype(jnp.bfloat16))
                total = total + jnp.dot(
                    jnp.concatenate(signals, axis=1),
                    jnp.concatenate(blocks, axis=0),
                    preferred_element_type=jnp.float32,
                )
            inner = total[:chunks] + total[chunks:] + skip_ref[channel] * mixed
            collected[pl.ds(channel, chunks, stride=per), :] = turn(inner, FIRST_SEQ)

        inner = collected[pl.ds(0, chunks * per), :]
        inner_ref[...] = inner.astype(jnp.bfloat16).reshape(inner_ref.shape)

    return call(
        kernel,
        [SMEM, VMEM],
        jax.ShapeDtypeStruct((chunks // 2, 2 * per, BLOCK), jnp.bfloat16),
        16 * per * chunks * chunks * BLOCK * BLOCK,
        [
            pltpu.VMEM(((chunks + 1) * rows, BLOCK), jnp.float32),
            pltpu.VMEM((2, 2 * chunks, BLOCK), jnp.float32),
            pltpu.VMEM(((chunks + 1) * per, BLOCK), jnp.float32),
        ],
        "causal_sum",
    )(skip, given)


def adjoint(given, back, skip):
    chunks, rows, _ = back.shape
    per = rows // 2
    wide_rows = given.shape[1]

    def kernel(skip_ref, given_ref, back_ref, out_ref, wide, grads, shifted, collected):
        wide[pl.ds(0, chunks * wide_rows), :] = (
            given_ref[...].astype(jnp.float32).reshape(chunks * wide_rows, BLOCK)
        )
        upper = upper_half()
        grads[pl.ds(0, chunks * rows), :] = (
            back_ref[...].astype(jnp.float32).reshape(chunks * rows, BLOCK)
        )
        shifted[pl.ds(chunks, chunks), :] = jnp.zeros((chunks, BLOCK), jnp.float32)

        @pl.loop(0, per)
        def _(channel):
            grad_inner = turn(grads[pl.ds(per + channel, chunks, stride=rows), :], -FIRST_SEQ)
            shifted[pl.ds(0, chunks), :] = grad_inner
            taps = turn(wide[pl.ds(2 * per + channel, chunks, stride=wide_rows), :], -FIRST_SEQ)
            before = jnp.zeros((BLOCK, BLOCK), jnp.float32)
            total = jnp.zeros((chunks, BLOCK), jnp.float32)
            for lag in range(0, chunks, 2):
                blocks, signals = [], []
                for one in (lag, lag + 1):
                    block, before = toeplitz_block(taps, one, before, upper)
                    blocks.append(block)
                    signals.append(shifted[one : one + chunks, :])
                total = total + lax.dot_general(
                    jnp.concatenate(signals, axis=1).astype(jnp.bfloat16),
                    jnp.concatenate(blocks, axis=1),
                    LANES,
                    preferred_element_type=jnp.float32,
                )
            grad_mixed = total + skip_ref[channel] * grad_inner
            collected[pl.ds(channel, chunks, stride=per), :] = turn(grad_mixed, FIRST_SEQ)

        mixed = collected[pl.ds(0, chunks * per), :]
        out_ref[...] = mixed.astype(jnp.bfloat16).reshape(out_ref.shape)

    return call(
        kernel,
        [SMEM, VMEM, VMEM],
        jax.ShapeDtypeStruct((chunks // 2, 2 * per, BLOCK), jnp.bfloat16),
        16 * per * chunks * chunks * BLOCK * BLOCK,
        [
            pltpu.VMEM(((chunks + 1) * wide_rows, BLOCK), jnp.float32),
            pltpu.VMEM(((chunks + 1) * rows, BLOCK), jnp.float32),
            pltpu.VMEM((2 * chunks, BLOCK), jnp.float32),
            pltpu.VMEM(((chunks + 1) * per, BLOCK), jnp.float32),
        ],
        "adjoint_sum",
    )(skip, given, back)


def per_device(projected, filters, skip, out_weight, cotangent):
    seq = lax.axis_size("seq")
    chan = lax.axis_size("chan")
    planes = chan // 2
    channels, count = filters.shape
    per = channels // seq
    half = lax.axis_index("chan") & 1
    own, other = half.reshape(1), (1 - half).reshape(1)
    along_z = [[2 * z + h for z in range(planes)] for h in range(2)]
    pairs = [(i, i ^ 1) for i in range(chan)]

    def exchange_seq(array):
        groups = [[(place + FIRST_SEQ) % seq for place in range(seq)]]
        return lax.all_to_all(array, "seq", 0, 0, tiled=True, axis_index_groups=groups)

    def exchange_z(array, first=0):
        groups = [group[first:] + group[:first] for group in along_z]
        return lax.all_to_all(array, "chan", 0, 0, tiled=True, axis_index_groups=groups)

    weight = out_weight.reshape(planes, 2, channels, out_weight.shape[1])
    share_other, packed = first(other, weight, cotangent, projected, filters, seq)
    received = lax.ppermute(share_other, "chan", pairs)
    given = exchange_seq(packed)
    share_own = partial_half(own, weight, cotangent, jnp.float32)
    skip_here = lax.dynamic_slice(skip, ((lax.axis_index("seq") - FIRST_SEQ) % seq * per,), (per,))
    inner = causal(given, skip_here)
    shares = exchange_z(total_share(share_own, received, FIRST_SUM), FIRST_SUM)
    packed, grad_gated = pack_middle(inner, shares, projected, seq)
    middle = exchange_seq(packed)
    gated = spread(middle, projected, planes)
    gated_half = exchange_z(gated, FIRST_GATED)
    grads_there = adjoint(given, middle, skip_here)
    plane = lax.axis_index("chan") >> 1
    grads_there, gated = lax.optimization_barrier((grads_there, gated))
    near = lax.ppermute(gated[0], "chan", pairs)
    grads_there, gated_half = lax.optimization_barrier((grads_there, gated_half))
    start = (plane - FIRST_GATED + 1) % planes
    gated_other = lax.ppermute(other_planes(start.reshape(1), gated_half), "chan", pairs)
    place = jnp.stack([half, plane])
    output, weight_other = project_half(place, gated_half, weight, FIRST_GATED)
    grads = exchange_seq(grads_there.reshape(seq, per, count))
    output = project_half((near,), gated_other, weight_other, FIRST_GATED, output)
    grads, output = lax.optimization_barrier((grads, output))
    grads = last_grads(grads.reshape(seq // 2, 2 * per, count), middle, grad_gated, projected)
    return output, grads


def solution(mesh):
    in_specs = (
        P(None, "chan", "seq"),
        P("chan", "seq"),
        P("chan"),
        P(None, "chan"),
        P("seq", "chan"),
    )
    out_specs = (P("seq", "chan"), P(None, "chan", "seq"))
    return jax.shard_map(
        per_device, mesh=mesh, in_specs=in_specs, out_specs=out_specs, check_vma=False
    )
```

```python
import jax
import jax.numpy as jnp
from jax import lax
from jax.experimental import pallas as pl
from jax.experimental.pallas import tpu as pltpu
from jax.sharding import PartitionSpec as P

BLOCK = 128
LANES = (((1,), (1,)), ((), ()))
ROWS = (((0,), (0,)), ((), ()))
VMEM_LIMIT = 8 << 20
FIRST_LIMIT = 54 << 20
FIRST_SUM = 6
FIRST_GATED = 5
FIRST_SEQ = 19
VMEM = pl.BlockSpec(memory_space=pltpu.VMEM)
HBM = pl.BlockSpec(memory_space=pltpu.HBM)
SMEM = pl.BlockSpec(memory_space=pltpu.SMEM)


def call(kernel, in_specs, out_shape, flops, scratch=(), name=None, limit=VMEM_LIMIT, out=VMEM):
    return pl.pallas_call(
        kernel,
        in_specs=in_specs,
        out_specs=jax.tree.map(lambda _: out, out_shape),
        out_shape=out_shape,
        scratch_shapes=list(scratch),
        compiler_params=pltpu.CompilerParams(vmem_limit_bytes=limit),
        cost_estimate=pl.CostEstimate(flops=flops, bytes_accessed=4 << 20, transcendentals=0),
        name=name,
    )


def partial_half(half, weight, cotangent, dtype):
    planes, _, rows, width = weight.shape
    count = cotangent.shape[0]

    def kernel(half_ref, weight_ref, cotangent_ref, out_ref):
        for plane in range(planes):
            out_ref[plane] = lax.dot_general(
                weight_ref[plane, half_ref[0]],
                cotangent_ref[...],
                LANES,
                preferred_element_type=jnp.float32,
            ).astype(dtype)

    return call(
        kernel,
        [SMEM, VMEM, VMEM],
        jax.ShapeDtypeStruct((planes, rows, count), dtype),
        2 * planes * rows * width * count,
        name="partial_grad_gated",
    )(half, weight, cotangent)


def total_share(share, received, first):
    planes = share.shape[0]

    def kernel(share_ref, received_ref, out_ref):
        for place in range(planes):
            plane = (place + first) % planes
            total = share_ref[plane] + received_ref[plane].astype(jnp.float32)
            out_ref[place] = total.astype(jnp.bfloat16)

    return call(
        kernel,
        [VMEM, VMEM],
        jax.ShapeDtypeStruct(share.shape, jnp.bfloat16),
        1 << 24,
        name="total_share",
    )(share, received)


def project_half(half, gated, weight, first, before=None):
    planes, rows, width = weight.shape[0], weight.shape[-2], weight.shape[-1]
    count = gated.shape[-1]
    result = jax.ShapeDtypeStruct((count, width), jnp.float32 if before is None else jnp.bfloat16)

    def early(half_ref, gated_ref, weight_ref, out_ref, kept_ref, moved):
        copies = [
            pltpu.make_async_copy(
                weight_ref.at[lax.rem(half_ref[1] + 1 + plane, planes), 1 - half_ref[0]],
                kept_ref.at[plane],
                moved.at[plane],
            )
            for plane in range(planes)
        ]
        for copy in copies:
            copy.start()
        total = jnp.zeros((count, width), jnp.float32)
        for plane in range(planes):
            total = total + lax.dot_general(
                gated_ref[plane],
                weight_ref[(plane + first) % planes, half_ref[0]],
                ROWS,
                preferred_element_type=jnp.float32,
            )
        out_ref[...] = total
        for copy in copies:
            copy.wait()

    def late(gated_ref, near_ref, weight_ref, before_ref, out_ref):
        others = planes - 1
        total = before_ref[...] + lax.dot_general(
            near_ref[...], weight_ref[others], ROWS, preferred_element_type=jnp.float32
        )
        total = total + lax.dot_general(
            gated_ref[...].reshape(others * rows, count),
            weight_ref[pl.ds(0, others)].reshape(others * rows, width),
            ROWS,
            preferred_element_type=jnp.float32,
        )
        out_ref[...] = total.astype(out_ref.dtype)

    flops = 2 * planes * rows * width * count
    if before is None:
        kept = jax.ShapeDtypeStruct((planes, rows, width), weight.dtype)
        return call(
            early,
            [SMEM, VMEM, VMEM],
            [result, kept],
            flops,
            [pltpu.SemaphoreType.DMA((planes,))],
            name="output_early",
        )(half, gated, weight)
    return call(late, [VMEM] * 4, result, flops, name="output_late")(gated, *half, weight, before)


def first(half, weight, cotangent, projected, filters, seq):
    planes, _, rows, width = weight.shape
    _, channels, count = projected.shape
    per = channels // seq

    def kernel(
        half_ref,
        weight_ref,
        cotangent_ref,
        projected_ref,
        filters_ref,
        share_ref,
        packed_ref,
        weight_here,
        cotangent_here,
        projected_here,
        filters_here,
        share_here,
        packed_here,
        arrived,
        left,
    ):
        places = [
            (projected_ref.at[pl.ds(1, 2)], projected_here),
            (filters_ref, filters_here),
            (cotangent_ref, cotangent_here),
        ]
        group = planes // 2
        places += [
            (weight_ref.at[pl.ds(start, group), half_ref[0]], weight_here.at[pl.ds(start, group)])
            for start in (0, group)
        ]
        copies = [
            pltpu.make_async_copy(source, target, arrived.at[i])
            for i, (source, target) in enumerate(places)
        ]
        for copy in copies:
            copy.start()
        copies[0].wait()
        copies[1].wait()
        parts = [projected_here[which].astype(jnp.float32) for which in range(2)]
        parts = [part.reshape(seq, per, count) for part in parts + [filters_here[...]]]
        packed_here[...] = jnp.concatenate(parts, axis=1).astype(jnp.bfloat16)
        leaving = [pltpu.make_async_copy(packed_here, packed_ref, left.at[2])]
        leaving[0].start()
        copies[2].wait()
        for place, start in enumerate((0, group)):
            copies[3 + place].wait()
            share = lax.dot_general(
                weight_here[pl.ds(start, group)].reshape(group * rows, width),
                cotangent_here[...],
                LANES,
                preferred_element_type=jnp.float32,
            )
            share_here[pl.ds(start, group)] = share.astype(jnp.bfloat16).reshape(group, rows, count)
            leaving.append(
                pltpu.make_async_copy(
                    share_here.at[pl.ds(start, group)],
                    share_ref.at[pl.ds(start, group)],
                    left.at[place],
                )
            )
            leaving[-1].start()
        for copy in leaving:
            copy.wait()

    return call(
        kernel,
        [SMEM, HBM, HBM, HBM, HBM],
        [
            jax.ShapeDtypeStruct((planes, rows, count), jnp.bfloat16),
            jax.ShapeDtypeStruct((seq, 3 * per, count), jnp.bfloat16),
        ],
        2 * planes * rows * width * count,
        [
            pltpu.VMEM((planes, rows, width), weight.dtype),
            pltpu.VMEM(cotangent.shape, cotangent.dtype),
            pltpu.VMEM((2, channels, count), projected.dtype),
            pltpu.VMEM(filters.shape, filters.dtype),
            pltpu.VMEM((planes, rows, count), jnp.bfloat16),
            pltpu.VMEM((seq, 3 * per, count), jnp.bfloat16),
            pltpu.SemaphoreType.DMA((5,)),
            pltpu.SemaphoreType.DMA((3,)),
        ],
        "first_share",
        FIRST_LIMIT,
        HBM,
    )(half, weight, cotangent, projected, filters)


def pack_middle(inner, shares, projected, seq):
    planes, channels, count = shares.shape
    per = channels // seq

    def kernel(inner_ref, shares_ref, projected_ref, out_ref, total_ref):
        total = shares_ref[0].astype(jnp.float32)
        for plane in range(1, planes):
            total = total + shares_ref[plane].astype(jnp.float32)
        total_ref[...] = total
        back = (total * projected_ref[0].astype(jnp.float32)).reshape(seq, per, count)
        there = inner_ref[...].astype(jnp.float32).reshape(seq, per, count)
        out_ref[...] = jnp.concatenate([there, back], axis=1).astype(jnp.bfloat16)

    return call(
        kernel,
        [VMEM, VMEM, VMEM],
        [
            jax.ShapeDtypeStruct((seq, 2 * per, count), jnp.bfloat16),
            jax.ShapeDtypeStruct((channels, count), jnp.float32),
        ],
        1 << 24,
        name="pack_middle",
    )(inner, shares, projected)


def spread(middle, projected, planes):
    seq, rows, count = middle.shape
    per = rows // 2

    def kernel(middle_ref, projected_ref, out_ref, gated, left):
        inner = middle_ref[...].astype(jnp.float32)[:, :per].reshape(seq * per, count)
        gated[...] = (projected_ref[0].astype(jnp.float32) * inner).astype(jnp.bfloat16)
        copies = [
            pltpu.make_async_copy(gated, out_ref.at[plane], left.at[plane])
            for plane in range(planes)
        ]
        for copy in copies:
            copy.start()
        for copy in copies:
            copy.wait()

    return call(
        kernel,
        [VMEM, VMEM],
        jax.ShapeDtypeStruct((planes, seq * per, count), jnp.bfloat16),
        1 << 24,
        [pltpu.VMEM((seq * per, count), jnp.bfloat16), pltpu.SemaphoreType.DMA((planes,))],
        "spread_gated",
        out=HBM,
    )(middle, projected)


def other_planes(start, gated):
    planes, channels, count = gated.shape

    def kernel(start_ref, gated_ref, out_ref, moved):
        copies = [
            pltpu.make_async_copy(
                gated_ref.at[lax.rem(start_ref[0] + place, planes)],
                out_ref.at[place],
                moved.at[place],
            )
            for place in range(planes - 1)
        ]
        for copy in copies:
            copy.start()
        for copy in copies:
            copy.wait()

    return call(
        kernel,
        [SMEM, VMEM],
        jax.ShapeDtypeStruct((planes - 1, channels, count), gated.dtype),
        1 << 22,
        [pltpu.SemaphoreType.DMA((planes - 1,))],
        "other_planes",
    )(start, gated)


def last_grads(grad_mixed, middle, grad_gated, projected):
    seq, rows, count = middle.shape
    per = rows // 2

    def kernel(grad_mixed_ref, middle_ref, grad_gated_ref, projected_ref, out_ref):
        inner = middle_ref[...].astype(jnp.float32)[:, :per].reshape(seq * per, count)
        mixed = grad_mixed_ref[...].astype(jnp.float32).reshape(seq * per, count)
        out_ref[0] = (grad_gated_ref[...] * inner).astype(jnp.bfloat16)
        out_ref[1] = (mixed * projected_ref[2].astype(jnp.float32)).astype(jnp.bfloat16)
        out_ref[2] = (mixed * projected_ref[1].astype(jnp.float32)).astype(jnp.bfloat16)

    return call(
        kernel,
        [VMEM, VMEM, VMEM, VMEM],
        jax.ShapeDtypeStruct((3, seq * per, count), jnp.bfloat16),
        1 << 24,
        name="last_grads",
    )(grad_mixed, middle, grad_gated, projected)


def turn(array, by):
    by = by % array.shape[0]
    return array if by == 0 else jnp.concatenate([array[by:], array[:by]], axis=0)


def toeplitz_block(taps, lag, before, upper):
    spread = jnp.broadcast_to(taps[lag : lag + 1, :], (BLOCK, BLOCK))
    turned = pltpu.roll(spread, 0, 1, stride=1, stride_axis=0)
    return jnp.where(upper, turned, before).astype(jnp.bfloat16), turned


def upper_half():
    sub, lane = (lax.broadcasted_iota(jnp.int32, (BLOCK, BLOCK), axis) for axis in range(2))
    return lane >= sub


def causal(given, skip):
    chunks, rows, _ = given.shape
    per = rows // 3

    def kernel(skip_ref, given_ref, inner_ref, wide, shifted, collected):
        wide[pl.ds(0, chunks * rows), :] = (
            given_ref[...].astype(jnp.float32).reshape(chunks * rows, BLOCK)
        )
        for part in range(2):
            shifted[part, pl.ds(0, chunks), :] = jnp.zeros((chunks, BLOCK), jnp.float32)
        upper = upper_half()

        @pl.loop(0, per)
        def _(channel):
            def take(which):
                return turn(wide[pl.ds(which * per + channel, chunks, stride=rows), :], -FIRST_SEQ)

            mixed, taps = take(0) * take(1), take(2)
            near = mixed.astype(jnp.bfloat16).astype(jnp.float32)
            shifted[0, pl.ds(chunks, chunks), :] = near
            shifted[1, pl.ds(chunks, chunks), :] = mixed - near
            before = jnp.zeros((BLOCK, BLOCK), jnp.float32)
            total = jnp.zeros((2 * chunks, BLOCK), jnp.float32)
            for lag in range(0, chunks, 2):
                blocks, signals = [], []
                for one in (lag, lag + 1):
                    block, before = toeplitz_block(taps, one, before, upper)
                    blocks.append(block)
                    parts = [shifted[part, chunks - one : 2 * chunks - one, :] for part in range(2)]
                    signals.append(jnp.concatenate(parts, axis=0).astype(jnp.bfloat16))
                total = total + jnp.dot(
                    jnp.concatenate(signals, axis=1),
                    jnp.concatenate(blocks, axis=0),
                    preferred_element_type=jnp.float32,
                )
            inner = total[:chunks] + total[chunks:] + skip_ref[channel] * mixed
            collected[pl.ds(channel, chunks, stride=per), :] = turn(inner, FIRST_SEQ)

        inner = collected[pl.ds(0, chunks * per), :]
        inner_ref[...] = inner.astype(jnp.bfloat16).reshape(inner_ref.shape)

    return call(
        kernel,
        [SMEM, VMEM],
        jax.ShapeDtypeStruct((chunks // 2, 2 * per, BLOCK), jnp.bfloat16),
        16 * per * chunks * chunks * BLOCK * BLOCK,
        [
            pltpu.VMEM(((chunks + 1) * rows, BLOCK), jnp.float32),
            pltpu.VMEM((2, 2 * chunks, BLOCK), jnp.float32),
            pltpu.VMEM(((chunks + 1) * per, BLOCK), jnp.float32),
        ],
        "causal_sum",
    )(skip, given)


def adjoint(given, back, skip):
    chunks, rows, _ = back.shape
    per = rows // 2
    wide_rows = given.shape[1]

    def kernel(skip_ref, given_ref, back_ref, out_ref, wide, grads, shifted, collected):
        wide[pl.ds(0, chunks * wide_rows), :] = (
            given_ref[...].astype(jnp.float32).reshape(chunks * wide_rows, BLOCK)
        )
        upper = upper_half()
        grads[pl.ds(0, chunks * rows), :] = (
            back_ref[...].astype(jnp.float32).reshape(chunks * rows, BLOCK)
        )
        shifted[pl.ds(chunks, chunks), :] = jnp.zeros((chunks, BLOCK), jnp.float32)

        @pl.loop(0, per)
        def _(channel):
            grad_inner = turn(grads[pl.ds(per + channel, chunks, stride=rows), :], -FIRST_SEQ)
            shifted[pl.ds(0, chunks), :] = grad_inner
            taps = turn(wide[pl.ds(2 * per + channel, chunks, stride=wide_rows), :], -FIRST_SEQ)
            before = jnp.zeros((BLOCK, BLOCK), jnp.float32)
            total = jnp.zeros((chunks, BLOCK), jnp.float32)
            for lag in range(0, chunks, 2):
                blocks, signals = [], []
                for one in (lag, lag + 1):
                    block, before = toeplitz_block(taps, one, before, upper)
                    blocks.append(block)
                    signals.append(shifted[one : one + chunks, :])
                total = total + lax.dot_general(
                    jnp.concatenate(signals, axis=1).astype(jnp.bfloat16),
                    jnp.concatenate(blocks, axis=1),
                    LANES,
                    preferred_element_type=jnp.float32,
                )
            grad_mixed = total + skip_ref[channel] * grad_inner
            collected[pl.ds(channel, chunks, stride=per), :] = turn(grad_mixed, FIRST_SEQ)

        mixed = collected[pl.ds(0, chunks * per), :]
        out_ref[...] = mixed.astype(jnp.bfloat16).reshape(out_ref.shape)

    return call(
        kernel,
        [SMEM, VMEM, VMEM],
        jax.ShapeDtypeStruct((chunks // 2, 2 * per, BLOCK), jnp.bfloat16),
        16 * per * chunks * chunks * BLOCK * BLOCK,
        [
            pltpu.VMEM(((chunks + 1) * wide_rows, BLOCK), jnp.float32),
            pltpu.VMEM(((chunks + 1) * rows, BLOCK), jnp.float32),
            pltpu.VMEM((2 * chunks, BLOCK), jnp.float32),
            pltpu.VMEM(((chunks + 1) * per, BLOCK), jnp.float32),
        ],
        "adjoint_sum",
    )(skip, given, back)


def per_device(projected, filters, skip, out_weight, cotangent):
    seq = lax.axis_size("seq")
    chan = lax.axis_size("chan")
    planes = chan // 2
    channels, count = filters.shape
    per = channels // seq
    half = lax.axis_index("chan") & 1
    own, other = half.reshape(1), (1 - half).reshape(1)
    along_z = [[2 * z + h for z in range(planes)] for h in range(2)]
    pairs = [(i, i ^ 1) for i in range(chan)]

    def exchange_seq(array):
        groups = [[(place + FIRST_SEQ) % seq for place in range(seq)]]
        return lax.all_to_all(array, "seq", 0, 0, tiled=True, axis_index_groups=groups)

    def exchange_z(array, first=0):
        groups = [group[first:] + group[:first] for group in along_z]
        return lax.all_to_all(array, "chan", 0, 0, tiled=True, axis_index_groups=groups)

    weight = out_weight.reshape(planes, 2, channels, out_weight.shape[1])
    share_other, packed = first(other, weight, cotangent, projected, filters, seq)
    received = lax.ppermute(share_other, "chan", pairs)
    given = exchange_seq(packed)
    share_own = partial_half(own, weight, cotangent, jnp.float32)
    skip_here = lax.dynamic_slice(skip, ((lax.axis_index("seq") - FIRST_SEQ) % seq * per,), (per,))
    inner = causal(given, skip_here)
    shares = exchange_z(total_share(share_own, received, FIRST_SUM), FIRST_SUM)
    packed, grad_gated = pack_middle(inner, shares, projected, seq)
    middle = exchange_seq(packed)
    gated = spread(middle, projected, planes)
    gated_half = exchange_z(gated, FIRST_GATED)
    grads_there = adjoint(given, middle, skip_here)
    plane = lax.axis_index("chan") >> 1
    grads_there, gated = lax.optimization_barrier((grads_there, gated))
    near = lax.ppermute(gated[0], "chan", pairs)
    grads_there, gated_half, near = lax.optimization_barrier((grads_there, gated_half, near))
    start = (plane - FIRST_GATED + 1) % planes
    gated_other = lax.ppermute(other_planes(start.reshape(1), gated_half), "chan", pairs)
    place = jnp.stack([half, plane])
    output, weight_other = project_half(place, gated_half, weight, FIRST_GATED)
    grads = exchange_seq(grads_there.reshape(seq, per, count))
    output = project_half((near,), gated_other, weight_other, FIRST_GATED, output)
    grads, output = lax.optimization_barrier((grads, output))
    grads = last_grads(grads.reshape(seq // 2, 2 * per, count), middle, grad_gated, projected)
    return output, grads


def solution(mesh):
    in_specs = (
        P(None, "chan", "seq"),
        P("chan", "seq"),
        P("chan"),
        P(None, "chan"),
        P("seq", "chan"),
    )
    out_specs = (P("seq", "chan"), P(None, "chan", "seq"))
    return jax.shard_map(
        per_device, mesh=mesh, in_specs=in_specs, out_specs=out_specs, check_vma=False
    )
```
